32 devices in a mesh: groups: 2 (over x), ctx: 16 (over z, y, core).
Axes of the slice: x: 2, y: 2, z: 4, core: 2. Of those that a mesh axis runs over, the one named last changes fastest.
Arguments:
- rotated_queries: bfloat16 [4096, 2048], P(('groups', 'ctx')), parts along dimension 0, may hold values from -6.5 to 6.5
- key_rows: bfloat16 [4096, 512], P(('groups', 'ctx')), parts along dimension 0, may hold values from -6.5 to 6.5
- value_matrix: bfloat16 [4096, 512], P(('groups', 'ctx')), parts along dimension 0, may hold values from -6 to 6
- doc_lengths: int32 [8], P('groups'), parts along dimension 0, may hold values from 1 to 1024, 2048 in all
Outputs:
- attended: bfloat16 [4096, 2048], P(('groups', 'ctx')), parts along dimension 0
The draws below stay inside these ranges and needn't reach their ends.
There are 2 independent parts, one for each index of `groups`. The reference program is written for one: setup_inputs(seed, part) draws one part's arguments, and reference() takes and returns one part's arrays. A program takes and returns all parts, laid end to end along the dimension named above; each array names one. Nothing has to cross between parts.
Inputs may be any that keep to these rules, and one draw needn't show every extreme that they name: `doc_lengths`: the 4 lengths of one part sum to 2048; the largest is exactly 1024.
All inputs are finite; a program needn't handle non-finite values.
Results may differ from the reference program's by a relative error of at most 0.005.
Values may be sent and summed in bfloat16 or wider, within the bound.
A program may use at most 128 MiB of HBM per device.

```python
import math
import jax
import jax.numpy as jnp
import numpy as np
from jax import lax

QUERY_HEADS = 16
KEY_VALUE_HEADS = 4
HEAD_WIDTH = 128
TOKENS_PER_SHARD = 128
DOCS = 4
LONGEST_LENGTH = 1024
CONTEXT_TOKENS = 2048


def starting_rows(key, width):
    normal_part = jnp.clip(jax.random.normal(key, (CONTEXT_TOKENS, width), jnp.float32), -4.0, 4.0)
    return normal_part


def draw_rotated_queries(key, part):
    output_values = starting_rows(jax.random.fold_in(key, 1), QUERY_HEADS * HEAD_WIDTH)
    return output_values.astype(jnp.bfloat16)


def draw_key_rows(key, part):
    output_values = starting_rows(jax.random.fold_in(key, 2), KEY_VALUE_HEADS * HEAD_WIDTH)
    return output_values.astype(jnp.bfloat16)


def steps_of(own_key, shape, pieces, smallest, high):
    loudness = 1.0
    for dim, shards_of in pieces:
        draws = jax.random.uniform(jax.random.fold_in(jax.random.fold_in(own_key, 6), dim), (shards_of,), jnp.float32, smallest / len(pieces), high / len(pieces))
        loudness = loudness * jnp.repeat(jnp.exp(draws), shape[dim] // shards_of).reshape((-1,) + (1,) * (len(shape) - 1 - dim))
    return loudness


def profile(amount, total, most, slope):
    weights = [(1 << 20) // math.isqrt(standing ** slope) + 1 for standing in range(2, amount + 1)]
    surplus, counts = total - most - (amount - 1), [1] * (amount - 1)
    while surplus > 0:
        free = [i for i in range(amount - 1) if counts[i] < most]
        whole, budget = sum([weights[i] for i in free]), surplus
        for i in free:
            addition = min(most - counts[i], max(1, budget * weights[i] // whole), surplus)
            counts[i] = counts[i] + addition
            surplus = surplus - addition
    return np.array([most] + counts)


def ragged(stream_key, count, total, limit, skew):
    if count == 2:
        one = jax.random.randint(stream_key, (), max(1, total - limit), min(limit, total - 1) + 1)
        return jnp.stack([one, total - one])
    sizes = jnp.asarray(profile(count, total, limit, skew), jnp.int32)
    twos = (count - 1) // 2
    source_of, receiver = sizes[1:1 + 2 * twos:2], sizes[2:2 + 2 * twos:2]
    margin = jnp.minimum(source_of - 1, limit - receiver)
    passed = jax.random.randint(jax.random.fold_in(stream_key, 1), (twos,), 0, 1 << 20) % (margin + 1)
    sizes = sizes.at[1:1 + 2 * twos:2].set(source_of - passed).at[2:2 + 2 * twos:2].set(receiver + passed)
    return sizes[jax.random.permutation(jax.random.fold_in(stream_key, 2), count)]


def gaussian(key, extent, scale, most, cuts=(), kind=jnp.bfloat16):
    result = jax.random.normal(key, extent, jnp.float32) * scale
    if len(cuts) > 0:
        result = steps_of(key, extent, cuts, -0.22, 0.18) * result
    return jnp.clip(result, min=-most, max=most).astype(kind)


def setup_inputs(seed: int = 0, part: int = 0) -> dict:
    seeds = jax.random.split(jax.random.key(seed), 5)
    part_keys = jax.random.split(jax.random.fold_in(seeds[4], part), 5)
    return {
        "rotated_queries": draw_rotated_queries(jax.random.fold_in(jax.random.fold_in(seeds[4], part), 71), part),
        "key_rows": draw_key_rows(jax.random.fold_in(jax.random.fold_in(seeds[4], part), 71), part),
        "value_matrix": gaussian(part_keys[2], (CONTEXT_TOKENS, KEY_VALUE_HEADS * HEAD_WIDTH), 1.0, 6.0, ((0, 16),)),
        "doc_lengths": ragged(part_keys[3], DOCS, CONTEXT_TOKENS, LONGEST_LENGTH, 2).astype(jnp.int32),
    }


def reference(rotated_queries, key_rows, value_matrix, doc_lengths):
    group_width = QUERY_HEADS // KEY_VALUE_HEADS
    positions = jnp.arange(CONTEXT_TOKENS, dtype=jnp.int32)
    doc_ends = jnp.cumsum(doc_lengths).astype(jnp.int32)
    starts_all = jnp.sum(jnp.where(doc_ends[None, :] <= positions[:, None], doc_lengths[None, :], 0), axis=1).astype(jnp.int32)
    padding_rows = jnp.zeros((LONGEST_LENGTH, KEY_VALUE_HEADS * HEAD_WIDTH), jnp.bfloat16)
    padded_keys = jnp.concatenate([padding_rows, key_rows], axis=0)
    padded_values = jnp.concatenate([padding_rows, value_matrix], axis=0)
    visible_window = LONGEST_LENGTH + TOKENS_PER_SHARD

    def one_block(block_number):
        first_index = (block_number * TOKENS_PER_SHARD).astype(jnp.int32)
        query_tile_rows = lax.dynamic_slice_in_dim(rotated_queries, first_index, TOKENS_PER_SHARD, 0).astype(jnp.float32).reshape(TOKENS_PER_SHARD, KEY_VALUE_HEADS, group_width, HEAD_WIDTH)
        key_tile_rows = lax.dynamic_slice_in_dim(padded_keys, first_index, visible_window, 0).astype(jnp.float32).reshape(visible_window, KEY_VALUE_HEADS, HEAD_WIDTH)
        value_tile_rows = lax.dynamic_slice_in_dim(padded_values, first_index, visible_window, 0).astype(jnp.float32).reshape(visible_window, KEY_VALUE_HEADS, HEAD_WIDTH)
        query_pos = first_index + jnp.arange(TOKENS_PER_SHARD, dtype=jnp.int32)
        query_start = lax.dynamic_slice_in_dim(starts_all, first_index, TOKENS_PER_SHARD, 0)
        key_pos = first_index - LONGEST_LENGTH + jnp.arange(visible_window, dtype=jnp.int32)
        scores = jnp.einsum("tkgd,skd->tkgs", query_tile_rows, key_tile_rows) * (HEAD_WIDTH ** -0.5)
        allowed = (key_pos[None, :] >= query_start[:, None]) & (key_pos[None, :] <= query_pos[:, None])
        allowed = allowed[:, None, None, :]
        scores = jnp.where(allowed, scores, jnp.float32(-1e30))
        row_max = jnp.max(scores, axis=-1, keepdims=True)
        weights = jnp.where(allowed, jnp.exp(scores - row_max), jnp.float32(0.0))
        total = jnp.sum(weights, axis=-1)
        weight_half = lax.optimization_barrier(weights.astype(jnp.bfloat16)).astype(jnp.float32)
        mixed = jnp.einsum("tkgs,skd->tkgd", weight_half, value_tile_rows) / total[..., None]
        return mixed.astype(jnp.bfloat16).reshape(TOKENS_PER_SHARD, QUERY_HEADS * HEAD_WIDTH)

    blocks = lax.map(one_block, jnp.arange(CONTEXT_TOKENS // TOKENS_PER_SHARD, dtype=jnp.int32))
    return blocks.reshape(CONTEXT_TOKENS, QUERY_HEADS * HEAD_WIDTH)
```

```python
import math

import jax
import jax.numpy as jnp
from jax import lax
from jax.experimental import pallas as pl
from jax.experimental.pallas import tpu as pltpu
from jax.sharding import PartitionSpec as P

QUERY_HEADS = 16
KEY_VALUE_HEADS = 4
HEAD_WIDTH = 128


masked_score = -1e30


def from_behind(shard, axis, by):
    peers = lax.axis_size(axis)
    pairs = [(i, i + by) for i in range(peers) if 0 <= i + by < peers]
    return lax.ppermute(shard, axis, pairs)


def doc_start_of(query_pos, doc_lengths):
    doc_ends = jnp.cumsum(doc_lengths)
    taken_lengths = jnp.where(doc_ends[None, :] <= query_pos[:, None], doc_lengths[None, :], 0)
    return jnp.sum(taken_lengths, axis=1)


def fold_block(state_now, block_slice, key_start, grouped_heads, query_pos, query_start):
    run_max, run_sum, accumulated = state_now
    token_count = block_slice.shape[1]
    local_keys = block_slice[0].reshape(token_count, KEY_VALUE_HEADS, HEAD_WIDTH)
    local_values = block_slice[1].reshape(token_count, KEY_VALUE_HEADS, HEAD_WIDTH)
    scores = jnp.einsum(
        "tkgd,skd->tkgs", grouped_heads, local_keys, preferred_element_type=jnp.float32
    ) * HEAD_WIDTH ** (-0.5)
    key_pos = key_start + jnp.arange(token_count, dtype=jnp.int32)
    allowed = (key_pos[None, :] >= query_start[:, None]) & (key_pos[None, :] <= query_pos[:, None])
    allowed = allowed[:, None, None, :]
    scores = jnp.where(allowed, scores, masked_score)
    new_max = jnp.maximum(run_max, jnp.max(scores, axis=-1))
    weights = jnp.where(allowed, jnp.exp(scores - new_max[..., None]), 0.0)
    factor = jnp.exp(run_max - new_max)
    run_sum = run_sum * factor + jnp.sum(weights, axis=-1)
    accumulated = accumulated * factor[..., None] + jnp.einsum(
        "tkgs,skd->tkgd",
        weights.astype(jnp.bfloat16),
        local_values,
        preferred_element_type=jnp.float32,
    )
    return (new_max, run_sum, accumulated)


def visit_block(state_now, block_slice, key_start, grouped_heads, query_pos, query_start):
    return fold_block(state_now, block_slice, key_start, grouped_heads, query_pos, query_start)


def per_device(rotated_queries, key_rows, value_matrix, doc_lengths):
    count_of_rows = rotated_queries.shape[0]
    span_count = lax.axis_size("ctx") // 2
    device_index = lax.axis_index("ctx")
    query_pos = device_index * count_of_rows + jnp.arange(count_of_rows, dtype=jnp.int32)
    query_start = doc_start_of(query_pos, doc_lengths)
    grouped_heads = rotated_queries.reshape(
        count_of_rows, KEY_VALUE_HEADS, QUERY_HEADS // KEY_VALUE_HEADS, HEAD_WIDTH
    )
    statistic_shape = (count_of_rows, KEY_VALUE_HEADS, QUERY_HEADS // KEY_VALUE_HEADS)
    state_now = (
        jnp.full(statistic_shape, masked_score, jnp.float32),
        jnp.zeros(statistic_shape, jnp.float32),
        jnp.zeros(statistic_shape + (HEAD_WIDTH,), jnp.float32),
    )
    own_block = jnp.stack([key_rows, value_matrix])
    state_now = visit_block(
        state_now, own_block, device_index * count_of_rows, grouped_heads, query_pos, query_start
    )
    stored = own_block[None]
    for level_number in range(16):
        held_count = stored.shape[0]
        send_count = min(held_count, span_count + 1 - held_count)
        if send_count > 0:
            arrived = from_behind(stored[:send_count], "ctx", held_count)

            def arrived_step(offset_number, inner_state, arrived=arrived, held_count=held_count):
                block_slice = lax.dynamic_index_in_dim(arrived, offset_number, 0, keepdims=False)
                key_start = (device_index - held_count - offset_number) * count_of_rows
                return visit_block(
                    inner_state, block_slice, key_start, grouped_heads, query_pos, query_start
                )

            state_now = lax.fori_loop(0, send_count, arrived_step, state_now)
            stored = jnp.concatenate([stored, arrived], axis=0)
    run_max, run_sum, accumulated = state_now
    result = accumulated / run_sum[..., None]
    return result.reshape(count_of_rows, QUERY_HEADS * HEAD_WIDTH).astype(jnp.bfloat16)


MESH = pl.DeviceIdType.MESH
GROUP_HEADS = QUERY_HEADS // KEY_VALUE_HEADS
EXP2_SCALE = math.log2(math.e) / math.sqrt(HEAD_WIDTH)

(Z1, Z2, C0, Y0, C0Y, C1, Y1, C1Y, C2, Y2, C2Y) = range(11)
HOPS = 11


def relay_kernel(
    lengths, q_hbm, k_hbm, v_hbm, o_hbm,
    held, q_rows, q_cols, row_max, row_sum, total, o_rows,
    own_sem, q_sem, o_sem, send_sem, recv_sem,
):
    tokens = q_hbm.shape[0]
    lanes = GROUP_HEADS * tokens
    group = lax.axis_index("groups")
    me = lax.axis_index("ctx")
    z, y, c = me // 4, (me // 2) % 2, me % 2
    up, down = me + 4, me - 4
    across = me + 2 - 4 * y
    twin = me + 1 - 2 * c

    def place(device):
        return (group, device)

    def slot(behind, head, from_y, from_c):
        return held.at[behind, head, from_y, :, from_c]

    def own_copies(head):
        columns = pl.ds(head * HEAD_WIDTH, HEAD_WIDTH)
        return [
            pltpu.make_async_copy(source.at[:, columns], held.at[0, head, y, which, c], own_sem.at[which, head])
            for which, source in enumerate((k_hbm, v_hbm))
        ]

    def hop(kind, head, source, target, device):
        return pltpu.make_async_remote_copy(
            src_ref=source, dst_ref=target, send_sem=send_sem.at[kind, head],
            recv_sem=recv_sem.at[kind, head], device_id=place(device), device_id_type=MESH,
        )

    def send(kind, head, behind, from_y, from_c, device, landing=None):
        landing = behind if landing is None else landing
        hop(kind, head, slot(behind, head, from_y, from_c), slot(landing, head, from_y, from_c), device).start()

    def arrived(kind, head, behind, from_y, from_c):
        here = slot(behind, head, from_y, from_c)
        hop(kind, head, here, here, twin).wait_recv()

    q_copy = pltpu.make_async_copy(q_hbm, q_rows, q_sem)
    for head in range(KEY_VALUE_HEADS):
        for copy in own_copies(head):
            copy.start()
    q_copy.start()

    barrier = pltpu.get_barrier_semaphore()

    def greet(device):
        pl.semaphore_signal(barrier, inc=1, device_id=place(device), device_id_type=MESH)

    greet(twin)
    greet(across)

    @pl.when(z < 3)
    def _():
        greet(up)

    @pl.when(z > 0)
    def _():
        greet(down)

    inner = (z > 0) & (z < 3)

    @pl.when(inner)
    def _():
        pl.semaphore_wait(barrier, 4)

    @pl.when(jnp.logical_not(inner))
    def _():
        pl.semaphore_wait(barrier, 3)

    for head in range(KEY_VALUE_HEADS):
        for copy in own_copies(head):
            copy.wait()

        @pl.when(z < 3)
        def _():
            send(Z1, head, 0, y, c, up, landing=1)

        @pl.when(y == 0)
        def _():
            send(Y0, head, 0, y, c, across)

        @pl.when(c == 0)
        def _():
            send(C0, head, 0, y, c, twin)

    q_copy.wait()
    for head in range(QUERY_HEADS):
        rows = q_rows[:, head * HEAD_WIDTH:(head + 1) * HEAD_WIDTH].astype(jnp.float32)
        at = head % GROUP_HEADS
        q_cols[head // GROUP_HEADS, :, at * tokens:(at + 1) * tokens] = rows.T.astype(jnp.bfloat16)

    query_pos = me * tokens + lax.broadcasted_iota(jnp.int32, (1, lanes), 1) % tokens
    doc_end = jnp.int32(0)
    query_start = jnp.zeros((1, lanes), jnp.int32)
    for doc in range(lengths.shape[0]):
        doc_end = doc_end + lengths[doc]
        query_start = query_start + jnp.where(doc_end <= query_pos, lengths[doc], 0)

    half = lanes // 2

    def attend(head, behind, from_y, from_c, pair, own=False):
        if pair:
            keys = held[behind, head, from_y, 0].reshape(2 * tokens, HEAD_WIDTH)
            values = held[behind, head, from_y, 1].reshape(2 * tokens, HEAD_WIDTH)
        else:
            keys = held[behind, head, from_y, 0, from_c]
            values = held[behind, head, from_y, 1, from_c]
        count = keys.shape[0]
        key_start = ((z - behind) * 4 + from_y * 2 + (0 if pair else from_c)) * tokens
        key_pos = key_start + lax.broadcasted_iota(jnp.int32, (count, half), 0)
        for part in range(2):
            cols = slice(part * half, (part + 1) * half)
            scores = jnp.dot(keys, q_cols[head, :, cols], preferred_element_type=jnp.float32)
            allowed = key_pos >= query_start[:, cols]
            if own:
                allowed = allowed & (key_pos <= query_pos[:, cols])
            scores = jnp.where(allowed, scores, masked_score)
            new_max = jnp.max(scores, axis=0, keepdims=True)
            if not own:
                old_max = row_max[head, :, cols]
                new_max = jnp.maximum(old_max, new_max)
            weights = jnp.exp2((scores - new_max) * EXP2_SCALE)
            weight_sum = jnp.sum(weights, axis=0, keepdims=True)
            mixed = lax.dot_general(
                values, weights.astype(jnp.bfloat16), (((0,), (0,)), ((), ())),
                preferred_element_type=jnp.float32,
            )
            if own:
                row_sum[head, :, cols] = weight_sum
                total[head, :, cols] = mixed
            else:
                factor = jnp.exp2((old_max - new_max) * EXP2_SCALE)
                row_sum[head, :, cols] = row_sum[head, :, cols] * factor + weight_sum
                total[head, :, cols] = total[head, :, cols] * factor + mixed
            row_max[head, :, cols] = new_max

    @pl.loop(0, KEY_VALUE_HEADS)
    def _(head):
        attend(head, 0, y, c, False, own=True)

    @pl.loop(0, KEY_VALUE_HEADS + 1)
    def _(step):
        @pl.when(step < KEY_VALUE_HEADS)
        def _():
            @pl.when(z >= 1)
            def _():
                arrived(Z1, step, 1, y, c)

                @pl.when(z < 3)
                def _():
                    send(Z2, step, 1, y, c, up, landing=2)

                send(Y1, step, 1, y, c, across)
                send(C1, step, 1, y, c, twin)

            @pl.when(y == 1)
            def _():
                arrived(Y0, step, 0, 0, c)
                send(C0Y, step, 0, 0, c, twin)

        @pl.when(step >= 1)
        def _():
            head = step - 1

            @pl.when(c == 1)
            def _():
                arrived(C0, head, 0, y, 0)
                attend(head, 0, y, 0, False)

            @pl.when(y == 1)
            def _():
                arrived(C0Y, head, 0, 0, 1 - c)
                attend(head, 0, 0, 0, True)

            @pl.when(z >= 1)
            def _():
                arrived(C1, head, 1, y, 1 - c)
                attend(head, 1, y, 0, True)

    @pl.loop(0, KEY_VALUE_HEADS + 1)
    def _(step):
        @pl.when(step < KEY_VALUE_HEADS)
        def _():
            @pl.when(z >= 1)
            def _():
                arrived(Y1, step, 1, 1 - y, c)
                send(C1Y, step, 1, 1 - y, c, twin)

            @pl.when(z >= 2)
            def _():
                arrived(Z2, step, 2, y, c)

                @pl.when(y == 1)
                def _():
                    send(Y2, step, 2, y, c, across)

                @pl.when(c == 1)
                def _():
                    send(C2, step, 2, y, c, twin)

        @pl.when(step >= 1)
        def _():
            head = step - 1

            @pl.when(z >= 1)
            def _():
                arrived(C1Y, head, 1, 1 - y, 1 - c)
                attend(head, 1, 1 - y, 0, True)

            @pl.when(z >= 2)
            def _():
                attend(head, 2, y, c, False)

                @pl.when(c == 0)
                def _():
                    arrived(C2, head, 2, y, 1)
                    attend(head, 2, y, 1, False)

    def o_copy(head):
        columns = pl.ds(pl.multiple_of(head * lanes, lanes), lanes)
        return pltpu.make_async_copy(o_rows.at[head], o_hbm.at[:, columns], o_sem.at[head])

    from_across = (z >= 2) & (y == 0)

    @pl.loop(0, KEY_VALUE_HEADS + 1)
    def _(step):
        @pl.when((step < KEY_VALUE_HEADS) & from_across)
        def _():
            arrived(Y2, step, 2, 1, c)
            send(C2Y, step, 2, 1, c, twin)

        @pl.when(step >= 1)
        def _():
            head = step - 1

            @pl.when(from_across)
            def _():
                arrived(C2Y, head, 2, 1, 1 - c)
                attend(head, 2, 1, 0, True)

            result = total[head] / row_sum[head]
            for at in range(GROUP_HEADS):
                own_cols = slice(at * tokens, (at + 1) * tokens)
                o_rows[head, :, at * HEAD_WIDTH:(at + 1) * HEAD_WIDTH] = result[:, own_cols].T.astype(jnp.bfloat16)
            o_copy(head).start()

    @pl.loop(0, KEY_VALUE_HEADS)
    def _(head):
        o_copy(head).wait()

        def sent(kind, behind, from_y, from_c):
            here = slot(behind, head, from_y, from_c)
            hop(kind, head, here, here, twin).wait_send()

        @pl.when(z < 3)
        def _():
            sent(Z1, 0, y, c)

        @pl.when(y == 0)
        def _():
            sent(Y0, 0, y, c)

        @pl.when(c == 0)
        def _():
            sent(C0, 0, y, c)

        @pl.when(y == 1)
        def _():
            sent(C0Y, 0, 0, c)

        @pl.when(z >= 1)
        def _():
            @pl.when(z < 3)
            def _():
                sent(Z2, 1, y, c)

            sent(Y1, 1, y, c)
            sent(C1, 1, y, c)
            sent(C1Y, 1, 1 - y, c)

        @pl.when((z >= 2) & (y == 1))
        def _():
            sent(Y2, 2, y, c)

        @pl.when((z >= 2) & (c == 1))
        def _():
            sent(C2, 2, y, c)

        @pl.when(from_across)
        def _():
            sent(C2Y, 2, 1, c)


def relay_attention(rotated_queries, key_rows, value_matrix, doc_lengths):
    tokens = rotated_queries.shape[0]
    lanes = GROUP_HEADS * tokens
    anywhere = pl.BlockSpec(memory_space=pl.ANY)
    pairs = 9 * tokens * tokens * QUERY_HEADS
    return pl.pallas_call(
        relay_kernel,
        out_shape=jax.ShapeDtypeStruct(rotated_queries.shape, jnp.bfloat16),
        in_specs=[pl.BlockSpec(memory_space=pltpu.SMEM), anywhere, anywhere, anywhere],
        out_specs=anywhere,
        scratch_shapes=[
            pltpu.VMEM((3, KEY_VALUE_HEADS, 2, 2, 2, tokens, HEAD_WIDTH), jnp.bfloat16),
            pltpu.VMEM(rotated_queries.shape, jnp.bfloat16),
            pltpu.VMEM((KEY_VALUE_HEADS, HEAD_WIDTH, lanes), jnp.bfloat16),
            pltpu.VMEM((KEY_VALUE_HEADS, 1, lanes), jnp.float32),
            pltpu.VMEM((KEY_VALUE_HEADS, 1, lanes), jnp.float32),
            pltpu.VMEM((KEY_VALUE_HEADS, HEAD_WIDTH, lanes), jnp.float32),
            pltpu.VMEM((KEY_VALUE_HEADS, tokens, GROUP_HEADS * HEAD_WIDTH), jnp.bfloat16),
            pltpu.SemaphoreType.DMA((2, KEY_VALUE_HEADS)),
            pltpu.SemaphoreType.DMA,
            pltpu.SemaphoreType.DMA((KEY_VALUE_HEADS,)),
            pltpu.SemaphoreType.DMA((HOPS, KEY_VALUE_HEADS)),
            pltpu.SemaphoreType.DMA((HOPS, KEY_VALUE_HEADS)),
        ],
        compiler_params=pltpu.CompilerParams(
            collective_id=0, has_side_effects=True, vmem_limit_bytes=32 * 1024 * 1024
        ),
        cost_estimate=pl.CostEstimate(
            flops=4 * pairs * HEAD_WIDTH, bytes_accessed=4 * 1024 * 1024, transcendentals=pairs
        ),
        name="relay_attention",
    )(doc_lengths, rotated_queries, key_rows, value_matrix)


def solution(mesh):
    in_specs = (
        P(("groups", "ctx"), None),
        P(("groups", "ctx"), None),
        P(("groups", "ctx"), None),
        P("groups"),
    )
    out_specs = P(("groups", "ctx"), None)
    body = relay_attention if mesh.shape["ctx"] == 16 else per_device
    return jax.shard_map(
        body, mesh=mesh, in_specs=in_specs, out_specs=out_specs, check_vma=False
    )
```

```python
import math

import jax
import jax.numpy as jnp
from jax import lax
from jax.experimental import pallas as pl
from jax.experimental.pallas import tpu as pltpu
from jax.sharding import PartitionSpec as P

QUERY_HEADS = 16
KEY_VALUE_HEADS = 4
HEAD_WIDTH = 128


masked_score = -1e30


def from_behind(shard, axis, by):
    peers = lax.axis_size(axis)
    pairs = [(i, i + by) for i in range(peers) if 0 <= i + by < peers]
    return lax.ppermute(shard, axis, pairs)


def doc_start_of(query_pos, doc_lengths):
    doc_ends = jnp.cumsum(doc_lengths)
    taken_lengths = jnp.where(doc_ends[None, :] <= query_pos[:, None], doc_lengths[None, :], 0)
    return jnp.sum(taken_lengths, axis=1)


def fold_block(state_now, block_slice, key_start, grouped_heads, query_pos, query_start):
    run_max, run_sum, accumulated = state_now
    token_count = block_slice.shape[1]
    local_keys = block_slice[0].reshape(token_count, KEY_VALUE_HEADS, HEAD_WIDTH)
    local_values = block_slice[1].reshape(token_count, KEY_VALUE_HEADS, HEAD_WIDTH)
    scores = jnp.einsum(
        "tkgd,skd->tkgs", grouped_heads, local_keys, preferred_element_type=jnp.float32
    ) * HEAD_WIDTH ** (-0.5)
    key_pos = key_start + jnp.arange(token_count, dtype=jnp.int32)
    allowed = (key_pos[None, :] >= query_start[:, None]) & (key_pos[None, :] <= query_pos[:, None])
    allowed = allowed[:, None, None, :]
    scores = jnp.where(allowed, scores, masked_score)
    new_max = jnp.maximum(run_max, jnp.max(scores, axis=-1))
    weights = jnp.where(allowed, jnp.exp(scores - new_max[..., None]), 0.0)
    factor = jnp.exp(run_max - new_max)
    run_sum = run_sum * factor + jnp.sum(weights, axis=-1)
    accumulated = accumulated * factor[..., None] + jnp.einsum(
        "tkgs,skd->tkgd",
        weights.astype(jnp.bfloat16),
        local_values,
        preferred_element_type=jnp.float32,
    )
    return (new_max, run_sum, accumulated)


def visit_block(state_now, block_slice, key_start, grouped_heads, query_pos, query_start):
    return fold_block(state_now, block_slice, key_start, grouped_heads, query_pos, query_start)


def per_device(rotated_queries, key_rows, value_matrix, doc_lengths):
    count_of_rows = rotated_queries.shape[0]
    span_count = lax.axis_size("ctx") // 2
    device_index = lax.axis_index("ctx")
    query_pos = device_index * count_of_rows + jnp.arange(count_of_rows, dtype=jnp.int32)
    query_start = doc_start_of(query_pos, doc_lengths)
    grouped_heads = rotated_queries.reshape(
        count_of_rows, KEY_VALUE_HEADS, QUERY_HEADS // KEY_VALUE_HEADS, HEAD_WIDTH
    )
    statistic_shape = (count_of_rows, KEY_VALUE_HEADS, QUERY_HEADS // KEY_VALUE_HEADS)
    state_now = (
        jnp.full(statistic_shape, masked_score, jnp.float32),
        jnp.zeros(statistic_shape, jnp.float32),
        jnp.zeros(statistic_shape + (HEAD_WIDTH,), jnp.float32),
    )
    own_block = jnp.stack([key_rows, value_matrix])
    state_now = visit_block(
        state_now, own_block, device_index * count_of_rows, grouped_heads, query_pos, query_start
    )
    stored = own_block[None]
    for level_number in range(16):
        held_count = stored.shape[0]
        send_count = min(held_count, span_count + 1 - held_count)
        if send_count > 0:
            arrived = from_behind(stored[:send_count], "ctx", held_count)

            def arrived_step(offset_number, inner_state, arrived=arrived, held_count=held_count):
                block_slice = lax.dynamic_index_in_dim(arrived, offset_number, 0, keepdims=False)
                key_start = (device_index - held_count - offset_number) * count_of_rows
                return visit_block(
                    inner_state, block_slice, key_start, grouped_heads, query_pos, query_start
                )

            state_now = lax.fori_loop(0, send_count, arrived_step, state_now)
            stored = jnp.concatenate([stored, arrived], axis=0)
    run_max, run_sum, accumulated = state_now
    result = accumulated / run_sum[..., None]
    return result.reshape(count_of_rows, QUERY_HEADS * HEAD_WIDTH).astype(jnp.bfloat16)


MESH = pl.DeviceIdType.MESH
GROUP_HEADS = QUERY_HEADS // KEY_VALUE_HEADS
EXP2_SCALE = math.log2(math.e) / math.sqrt(HEAD_WIDTH)

(Z1, Z2, C0, Y0, C0Y, C1, Y1, C1Y, C2, Y2, C2Y) = range(11)
HOPS = 11


def relay_kernel(
    lengths_hbm, q_hbm, k_hbm, v_hbm, o_hbm,
    lengths, held, q_rows, q_cols, row_max, row_sum, total, o_rows,
    lengths_sem, own_sem, q_sem, o_sem, send_sem, recv_sem,
):
    tokens = q_hbm.shape[0]
    lanes = GROUP_HEADS * tokens
    group = lax.axis_index("groups")
    me = lax.axis_index("ctx")
    z, y, c = me // 4, (me // 2) % 2, me % 2
    up, down = me + 4, me - 4
    across = me + 2 - 4 * y
    twin = me + 1 - 2 * c

    def place(device):
        return (group, device)

    def slot(behind, head, from_y, from_c):
        return held.at[behind, head, from_y, :, from_c]

    def own_copies(head):
        columns = pl.ds(head * HEAD_WIDTH, HEAD_WIDTH)
        return [
            pltpu.make_async_copy(source.at[:, columns], held.at[0, head, y, which, c], own_sem.at[which, head])
            for which, source in enumerate((k_hbm, v_hbm))
        ]

    def hop(kind, head, source, target, device):
        return pltpu.make_async_remote_copy(
            src_ref=source, dst_ref=target, send_sem=send_sem.at[kind, head],
            recv_sem=recv_sem.at[kind, head], device_id=place(device), device_id_type=MESH,
        )

    def send(kind, head, behind, from_y, from_c, device, landing=None):
        landing = behind if landing is None else landing
        hop(kind, head, slot(behind, head, from_y, from_c), slot(landing, head, from_y, from_c), device).start()

    def arrived(kind, head, behind, from_y, from_c):
        here = slot(behind, head, from_y, from_c)
        hop(kind, head, here, here, twin).wait_recv()

    q_copy = pltpu.make_async_copy(q_hbm, q_rows, q_sem)
    lengths_copy = pltpu.make_async_copy(lengths_hbm, lengths, lengths_sem)
    for head in range(KEY_VALUE_HEADS):
        for copy in own_copies(head):
            copy.start()
    q_copy.start()
    lengths_copy.start()

    barrier = pltpu.get_barrier_semaphore()

    def greet(device):
        pl.semaphore_signal(barrier, inc=1, device_id=place(device), device_id_type=MESH)

    greet(twin)
    greet(across)

    @pl.when(z < 3)
    def _():
        greet(up)

    @pl.when(z > 0)
    def _():
        greet(down)

    inner = (z > 0) & (z < 3)

    @pl.when(inner)
    def _():
        pl.semaphore_wait(barrier, 4)

    @pl.when(jnp.logical_not(inner))
    def _():
        pl.semaphore_wait(barrier, 3)

    for head in range(KEY_VALUE_HEADS):
        for copy in own_copies(head):
            copy.wait()

        @pl.when(z < 3)
        def _():
            send(Z1, head, 0, y, c, up, landing=1)

        @pl.when(y == 0)
        def _():
            send(Y0, head, 0, y, c, across)

        send(C0, head, 0, y, c, twin)

    lengths_copy.wait()
    q_copy.wait()
    for head in range(QUERY_HEADS):
        rows = q_rows[:, head * HEAD_WIDTH:(head + 1) * HEAD_WIDTH].astype(jnp.float32)
        at = head % GROUP_HEADS
        q_cols[head // GROUP_HEADS, :, at * tokens:(at + 1) * tokens] = rows.T.astype(jnp.bfloat16)

    query_pos = me * tokens + lax.broadcasted_iota(jnp.int32, (1, lanes), 1) % tokens
    doc_end = jnp.int32(0)
    query_start = jnp.zeros((1, lanes), jnp.int32)
    for doc in range(lengths.shape[0]):
        doc_end = doc_end + lengths[doc]
        query_start = query_start + jnp.where(doc_end <= query_pos, lengths[doc], 0)

    half = lanes // 2

    def attend(head, behind, from_y, first=False):
        keys = held[behind, head, from_y, 0].reshape(2 * tokens, HEAD_WIDTH)
        values = held[behind, head, from_y, 1].reshape(2 * tokens, HEAD_WIDTH)
        key_start = ((z - behind) * 4 + from_y * 2) * tokens
        key_pos = key_start + lax.broadcasted_iota(jnp.int32, (2 * tokens, half), 0)
        for part in range(2):
            cols = slice(part * half, (part + 1) * half)
            scores = jnp.dot(keys, q_cols[head, :, cols], preferred_element_type=jnp.float32)
            allowed = key_pos >= query_start[:, cols]
            if first:
                allowed = allowed & (key_pos <= query_pos[:, cols])
            scores = jnp.where(allowed, scores, masked_score)
            new_max = jnp.max(scores, axis=0, keepdims=True)
            if not first:
                old_max = row_max[head, :, cols]
                new_max = jnp.maximum(old_max, new_max)
            weights = jnp.exp2((scores - new_max) * EXP2_SCALE)
            weight_sum = jnp.sum(weights, axis=0, keepdims=True)
            mixed = lax.dot_general(
                values, weights.astype(jnp.bfloat16), (((0,), (0,)), ((), ())),
                preferred_element_type=jnp.float32,
            )
            if first:
                row_sum[head, :, cols] = weight_sum
                total[head, :, cols] = mixed
            else:
                factor = jnp.exp2((old_max - new_max) * EXP2_SCALE)
                row_sum[head, :, cols] = row_sum[head, :, cols] * factor + weight_sum
                total[head, :, cols] = total[head, :, cols] * factor + mixed
            row_max[head, :, cols] = new_max

    @pl.loop(0, KEY_VALUE_HEADS + 1)
    def _(step):
        @pl.when(step < KEY_VALUE_HEADS)
        def _():
            @pl.when(z >= 1)
            def _():
                arrived(Z1, step, 1, y, c)

                @pl.when(z < 3)
                def _():
                    send(Z2, step, 1, y, c, up, landing=2)

                send(Y1, step, 1, y, c, across)
                send(C1, step, 1, y, c, twin)

            @pl.when(y == 1)
            def _():
                arrived(Y0, step, 0, 0, c)
                send(C0Y, step, 0, 0, c, twin)

            arrived(C0, step, 0, y, 1 - c)
            attend(step, 0, y, first=True)

        @pl.when(step >= 1)
        def _():
            head = step - 1

            @pl.when(y == 1)
            def _():
                arrived(C0Y, head, 0, 0, 1 - c)
                attend(head, 0, 0)

            @pl.when(z >= 1)
            def _():
                arrived(C1, head, 1, y, 1 - c)
                attend(head, 1, y)

    def o_copy(head):
        columns = pl.ds(pl.multiple_of(head * lanes, lanes), lanes)
        return pltpu.make_async_copy(o_rows.at[head], o_hbm.at[:, columns], o_sem.at[head])

    from_across = (z >= 2) & (y == 0)

    @pl.loop(0, KEY_VALUE_HEADS + 2)
    def _(step):
        @pl.when(step < KEY_VALUE_HEADS)
        def _():
            @pl.when(z >= 1)
            def _():
                arrived(Y1, step, 1, 1 - y, c)
                send(C1Y, step, 1, 1 - y, c, twin)

            @pl.when(z >= 2)
            def _():
                arrived(Z2, step, 2, y, c)

                @pl.when(y == 1)
                def _():
                    send(Y2, step, 2, y, c, across)

                send(C2, step, 2, y, c, twin)

        @pl.when((step >= 1) & (step <= KEY_VALUE_HEADS))
        def _():
            head = step - 1

            @pl.when(z >= 1)
            def _():
                arrived(C1Y, head, 1, 1 - y, 1 - c)
                attend(head, 1, 1 - y)

            @pl.when(z >= 2)
            def _():
                arrived(C2, head, 2, y, 1 - c)
                attend(head, 2, y)

            @pl.when(from_across)
            def _():
                arrived(Y2, head, 2, 1, c)
                send(C2Y, head, 2, 1, c, twin)

        @pl.when(step >= 2)
        def _():
            head = step - 2

            @pl.when(from_across)
            def _():
                arrived(C2Y, head, 2, 1, 1 - c)
                attend(head, 2, 1)

            result = total[head] / row_sum[head]
            for at in range(GROUP_HEADS):
                own_cols = slice(at * tokens, (at + 1) * tokens)
                o_rows[head, :, at * HEAD_WIDTH:(at + 1) * HEAD_WIDTH] = result[:, own_cols].T.astype(jnp.bfloat16)
            o_copy(head).start()

    @pl.loop(0, KEY_VALUE_HEADS)
    def _(head):
        o_copy(head).wait()

        def sent(kind, behind, from_y, from_c):
            here = slot(behind, head, from_y, from_c)
            hop(kind, head, here, here, twin).wait_send()

        @pl.when(z < 3)
        def _():
            sent(Z1, 0, y, c)

        @pl.when(y == 0)
        def _():
            sent(Y0, 0, y, c)

        sent(C0, 0, y, c)

        @pl.when(y == 1)
        def _():
            sent(C0Y, 0, 0, c)

        @pl.when(z >= 1)
        def _():
            @pl.when(z < 3)
            def _():
                sent(Z2, 1, y, c)

            sent(Y1, 1, y, c)
            sent(C1, 1, y, c)
            sent(C1Y, 1, 1 - y, c)

        @pl.when((z >= 2) & (y == 1))
        def _():
            sent(Y2, 2, y, c)

        @pl.when(z >= 2)
        def _():
            sent(C2, 2, y, c)

        @pl.when(from_across)
        def _():
            sent(C2Y, 2, 1, c)


def relay_attention(rotated_queries, key_rows, value_matrix, doc_lengths):
    tokens = rotated_queries.shape[0]
    lanes = GROUP_HEADS * tokens
    in_hbm = pl.BlockSpec(memory_space=pltpu.HBM)
    pairs = 9 * tokens * tokens * QUERY_HEADS
    return pl.pallas_call(
        relay_kernel,
        out_shape=jax.ShapeDtypeStruct(rotated_queries.shape, jnp.bfloat16),
        in_specs=[in_hbm] * 4,
        out_specs=pl.BlockSpec(memory_space=pl.ANY),
        scratch_shapes=[
            pltpu.SMEM(doc_lengths.shape, jnp.int32),
            pltpu.VMEM((3, KEY_VALUE_HEADS, 2, 2, 2, tokens, HEAD_WIDTH), jnp.bfloat16),
            pltpu.VMEM(rotated_queries.shape, jnp.bfloat16),
            pltpu.VMEM((KEY_VALUE_HEADS, HEAD_WIDTH, lanes), jnp.bfloat16),
            pltpu.VMEM((KEY_VALUE_HEADS, 1, lanes), jnp.float32),
            pltpu.VMEM((KEY_VALUE_HEADS, 1, lanes), jnp.float32),
            pltpu.VMEM((KEY_VALUE_HEADS, HEAD_WIDTH, lanes), jnp.float32),
            pltpu.VMEM((KEY_VALUE_HEADS, tokens, GROUP_HEADS * HEAD_WIDTH), jnp.bfloat16),
            pltpu.SemaphoreType.DMA,
            pltpu.SemaphoreType.DMA((2, KEY_VALUE_HEADS)),
            pltpu.SemaphoreType.DMA,
            pltpu.SemaphoreType.DMA((KEY_VALUE_HEADS,)),
            pltpu.SemaphoreType.DMA((HOPS, KEY_VALUE_HEADS)),
            pltpu.SemaphoreType.DMA((HOPS, KEY_VALUE_HEADS)),
        ],
        compiler_params=pltpu.CompilerParams(
            collective_id=0, has_side_effects=True, vmem_limit_bytes=32 * 1024 * 1024
        ),
        cost_estimate=pl.CostEstimate(
            flops=4 * pairs * HEAD_WIDTH, bytes_accessed=4 * 1024 * 1024, transcendentals=pairs
        ),
        name="relay_attention",
    )(doc_lengths, rotated_queries, key_rows, value_matrix)


def solution(mesh):
    in_specs = (
        P(("groups", "ctx"), None),
        P(("groups", "ctx"), None),
        P(("groups", "ctx"), None),
        P("groups"),
    )
    out_specs = P(("groups", "ctx"), None)
    body = relay_attention if mesh.shape["ctx"] == 16 else per_device
    return jax.shard_map(
        body, mesh=mesh, in_specs=in_specs, out_specs=out_specs, check_vma=False
    )
```

```python
import math

import jax
import jax.numpy as jnp
from jax import lax
from jax.experimental import pallas as pl
from jax.experimental.pallas import tpu as pltpu
from jax.sharding import PartitionSpec as P

QUERY_HEADS = 16
KEY_VALUE_HEADS = 4
HEAD_WIDTH = 128


masked_score = -1e30


def from_behind(shard, axis, by):
    peers = lax.axis_size(axis)
    pairs = [(i, i + by) for i in range(peers) if 0 <= i + by < peers]
    return lax.ppermute(shard, axis, pairs)


def doc_start_of(query_pos, doc_lengths):
    doc_ends = jnp.cumsum(doc_lengths)
    taken_lengths = jnp.where(doc_ends[None, :] <= query_pos[:, None], doc_lengths[None, :], 0)
    return jnp.sum(taken_lengths, axis=1)


def fold_block(state_now, block_slice, key_start, grouped_heads, query_pos, query_start):
    run_max, run_sum, accumulated = state_now
    token_count = block_slice.shape[1]
    local_keys = block_slice[0].reshape(token_count, KEY_VALUE_HEADS, HEAD_WIDTH)
    local_values = block_slice[1].reshape(token_count, KEY_VALUE_HEADS, HEAD_WIDTH)
    scores = jnp.einsum(
        "tkgd,skd->tkgs", grouped_heads, local_keys, preferred_element_type=jnp.float32
    ) * HEAD_WIDTH ** (-0.5)
    key_pos = key_start + jnp.arange(token_count, dtype=jnp.int32)
    allowed = (key_pos[None, :] >= query_start[:, None]) & (key_pos[None, :] <= query_pos[:, None])
    allowed = allowed[:, None, None, :]
    scores = jnp.where(allowed, scores, masked_score)
    new_max = jnp.maximum(run_max, jnp.max(scores, axis=-1))
    weights = jnp.where(allowed, jnp.exp(scores - new_max[..., None]), 0.0)
    factor = jnp.exp(run_max - new_max)
    run_sum = run_sum * factor + jnp.sum(weights, axis=-1)
    accumulated = accumulated * factor[..., None] + jnp.einsum(
        "tkgs,skd->tkgd",
        weights.astype(jnp.bfloat16),
        local_values,
        preferred_element_type=jnp.float32,
    )
    return (new_max, run_sum, accumulated)


def visit_block(state_now, block_slice, key_start, grouped_heads, query_pos, query_start):
    return fold_block(state_now, block_slice, key_start, grouped_heads, query_pos, query_start)


def per_device(rotated_queries, key_rows, value_matrix, doc_lengths):
    count_of_rows = rotated_queries.shape[0]
    span_count = lax.axis_size("ctx") // 2
    device_index = lax.axis_index("ctx")
    query_pos = device_index * count_of_rows + jnp.arange(count_of_rows, dtype=jnp.int32)
    query_start = doc_start_of(query_pos, doc_lengths)
    grouped_heads = rotated_queries.reshape(
        count_of_rows, KEY_VALUE_HEADS, QUERY_HEADS // KEY_VALUE_HEADS, HEAD_WIDTH
    )
    statistic_shape = (count_of_rows, KEY_VALUE_HEADS, QUERY_HEADS // KEY_VALUE_HEADS)
    state_now = (
        jnp.full(statistic_shape, masked_score, jnp.float32),
        jnp.zeros(statistic_shape, jnp.float32),
        jnp.zeros(statistic_shape + (HEAD_WIDTH,), jnp.float32),
    )
    own_block = jnp.stack([key_rows, value_matrix])
    state_now = visit_block(
        state_now, own_block, device_index * count_of_rows, grouped_heads, query_pos, query_start
    )
    stored = own_block[None]
    for level_number in range(16):
        held_count = stored.shape[0]
        send_count = min(held_count, span_count + 1 - held_count)
        if send_count > 0:
            arrived = from_behind(stored[:send_count], "ctx", held_count)

            def arrived_step(offset_number, inner_state, arrived=arrived, held_count=held_count):
                block_slice = lax.dynamic_index_in_dim(arrived, offset_number, 0, keepdims=False)
                key_start = (device_index - held_count - offset_number) * count_of_rows
                return visit_block(
                    inner_state, block_slice, key_start, grouped_heads, query_pos, query_start
                )

            state_now = lax.fori_loop(0, send_count, arrived_step, state_now)
            stored = jnp.concatenate([stored, arrived], axis=0)
    run_max, run_sum, accumulated = state_now
    result = accumulated / run_sum[..., None]
    return result.reshape(count_of_rows, QUERY_HEADS * HEAD_WIDTH).astype(jnp.bfloat16)


MESH = pl.DeviceIdType.MESH
GROUP_HEADS = QUERY_HEADS // KEY_VALUE_HEADS
EXP2_SCALE = math.log2(math.e) / math.sqrt(HEAD_WIDTH)

(Z1, Z2, C0, Y0, C0Y, C1, Y1, C1Y, C2, Y2, C2Y) = range(11)
HOPS = 11
HEADS_AT_ONCE = 2


def relay_kernel(
    lengths_hbm, q_hbm, k_hbm, v_hbm, o_hbm,
    lengths, held, q_rows, v_rows, q_cols, row_max, row_sum, total, o_rows,
    lengths_sem, k_sem, v_sem, q_sem, o_sem, send_sem, recv_sem,
):
    tokens = q_hbm.shape[0]
    lanes = GROUP_HEADS * tokens
    group = lax.axis_index("groups")
    me = lax.axis_index("ctx")
    z, y, c = me // 4, (me // 2) % 2, me % 2
    up, down = me + 4, me - 4
    across = me + 2 - 4 * y
    twin = me + 1 - 2 * c

    def place(device):
        return (group, device)

    def slot(behind, head, from_y, from_c):
        return held.at[behind, head, from_y, :, from_c]

    def k_copy(head):
        columns = pl.ds(head * HEAD_WIDTH, HEAD_WIDTH)
        return pltpu.make_async_copy(k_hbm.at[:, columns], held.at[0, head, y, 0, c], k_sem.at[head])

    def v_copy(head):
        columns = pl.ds(head * HEAD_WIDTH, HEAD_WIDTH)
        return pltpu.make_async_copy(v_hbm.at[:, columns], v_rows.at[head], v_sem.at[head])

    def hop(kind, head, source, target, device):
        return pltpu.make_async_remote_copy(
            src_ref=source, dst_ref=target, send_sem=send_sem.at[kind, head],
            recv_sem=recv_sem.at[kind, head], device_id=place(device), device_id_type=MESH,
        )

    def send(kind, head, behind, from_y, from_c, device, landing=None):
        landing = behind if landing is None else landing
        hop(kind, head, slot(behind, head, from_y, from_c), slot(landing, head, from_y, from_c), device).start()

    def arrived(kind, head, behind, from_y, from_c):
        here = slot(behind, head, from_y, from_c)
        hop(kind, head, here, here, twin).wait_recv()

    q_copy = pltpu.make_async_copy(q_hbm, q_rows, q_sem)
    lengths_copy = pltpu.make_async_copy(lengths_hbm, lengths, lengths_sem)
    for head in range(KEY_VALUE_HEADS):
        v_copy(head).start()
        k_copy(head).start()
    q_copy.start()
    lengths_copy.start()

    barrier = pltpu.get_barrier_semaphore()

    def greet(device):
        pl.semaphore_signal(barrier, inc=1, device_id=place(device), device_id_type=MESH)

    greet(twin)
    greet(across)

    @pl.when(z < 3)
    def _():
        greet(up)

    @pl.when(z > 0)
    def _():
        greet(down)

    for head in range(KEY_VALUE_HEADS):
        v_copy(head).wait()
        held[0, head, y, 1, c] = v_rows[head].astype(jnp.float32).T.astype(jnp.bfloat16)

    inner = (z > 0) & (z < 3)

    @pl.when(inner)
    def _():
        pl.semaphore_wait(barrier, 4)

    @pl.when(jnp.logical_not(inner))
    def _():
        pl.semaphore_wait(barrier, 3)

    for head in range(KEY_VALUE_HEADS):
        k_copy(head).wait()

        @pl.when(z < 3)
        def _():
            send(Z1, head, 0, y, c, up, landing=1)

        @pl.when(y == 0)
        def _():
            send(Y0, head, 0, y, c, across)

        @pl.when(c == 0)
        def _():
            send(C0, head, 0, y, c, twin)

    lengths_copy.wait()
    q_copy.wait()
    for head in range(QUERY_HEADS):
        rows = q_rows[:, head * HEAD_WIDTH:(head + 1) * HEAD_WIDTH].astype(jnp.float32)
        at = head % GROUP_HEADS
        q_cols[head // GROUP_HEADS, :, at * tokens:(at + 1) * tokens] = rows.T.astype(jnp.bfloat16)

    query_pos = me * tokens + lax.broadcasted_iota(jnp.int32, (1, lanes), 1) % tokens
    doc_end = jnp.int32(0)
    query_start = jnp.zeros((1, lanes), jnp.int32)
    for doc in range(lengths.shape[0]):
        doc_end = doc_end + lengths[doc]
        query_start = query_start + jnp.where(doc_end <= query_pos, lengths[doc], 0)

    half = lanes // 2
    chains = [(at, part) for at in range(HEADS_AT_ONCE) for part in range(2)]

    def attend(heads, behind, from_y, from_c, first=False):
        count = tokens if from_c is not None else 2 * tokens
        key_start = ((z - behind) * 4 + from_y * 2 + (0 if from_c is None else from_c)) * tokens
        key_pos = lax.broadcasted_iota(jnp.int32, (count, half), 0)

        def cols_of(part):
            return slice(part * half, (part + 1) * half)

        def scores_of(chain):
            at, part = chain
            if from_c is None:
                keys = held[behind, heads + at, from_y, 0].reshape(count, HEAD_WIDTH)
            else:
                keys = held[behind, heads + at, from_y, 0, from_c]
            return jnp.dot(keys, q_cols[heads + at, :, cols_of(part)], preferred_element_type=jnp.float32)

        def fold(chain, scores):
            at, part = chain
            head, cols = heads + at, cols_of(part)
            if from_c is None:
                values = jnp.concatenate(
                    [held[behind, head, from_y, 1, 0], held[behind, head, from_y, 1, 1]], axis=1
                )
            else:
                values = held[behind, head, from_y, 1, from_c]
            allowed = key_pos >= query_start[:, cols] - key_start
            if first:
                allowed = allowed & (key_pos <= query_pos[:, cols] - key_start)
            scores = jnp.where(allowed, scores, masked_score)
            new_max = jnp.max(scores, axis=0, keepdims=True)
            if not first:
                old_max = row_max[head, :, cols]
                new_max = jnp.maximum(old_max, new_max)
            weights = jnp.exp2((scores - new_max) * EXP2_SCALE)
            weight_sum = jnp.sum(weights, axis=0, keepdims=True)
            mixed = jnp.dot(values, weights.astype(jnp.bfloat16), preferred_element_type=jnp.float32)
            if first:
                row_sum[head, :, cols] = weight_sum
                total[head, :, cols] = mixed
            else:
                factor = jnp.exp2((old_max - new_max) * EXP2_SCALE)
                row_sum[head, :, cols] = row_sum[head, :, cols] * factor + weight_sum
                total[head, :, cols] = total[head, :, cols] * factor + mixed
            row_max[head, :, cols] = new_max

        ready = scores_of(chains[0])
        for number, chain in enumerate(chains):
            scores = ready
            if number + 1 < len(chains):
                ready = scores_of(chains[number + 1])
            fold(chain, scores)

    def each(heads, wait):
        for at in range(HEADS_AT_ONCE):
            wait(heads + at)

    def pass_on_first(head):
        @pl.when(z >= 1)
        def _():
            arrived(Z1, head, 1, y, c)

            @pl.when(z < 3)
            def _():
                send(Z2, head, 1, y, c, up, landing=2)

            send(Y1, head, 1, y, c, across)
            send(C1, head, 1, y, c, twin)

        @pl.when(y == 1)
        def _():
            arrived(Y0, head, 0, 0, c)
            send(C0Y, head, 0, 0, c, twin)

    steps = KEY_VALUE_HEADS // HEADS_AT_ONCE

    @pl.loop(0, steps + 1)
    def _(step):
        @pl.when(step < steps)
        def _():
            pass_on_first(step * HEADS_AT_ONCE)

        @pl.when(step >= 1)
        def _():
            heads = (step - 1) * HEADS_AT_ONCE

            @pl.when(y == 1)
            def _():
                each(heads, lambda head: arrived(C0Y, head, 0, 0, 1 - c))
                attend(heads, 0, 0, None)

            @pl.when(z >= 1)
            def _():
                each(heads, lambda head: arrived(C1, head, 1, y, 1 - c))
                attend(heads, 1, y, None)

        @pl.when(step < steps)
        def _():
            heads = step * HEADS_AT_ONCE
            for at in range(1, HEADS_AT_ONCE):
                pass_on_first(heads + at)

            @pl.when(c == 0)
            def _():
                attend(heads, 0, y, 0, first=True)

            @pl.when(c == 1)
            def _():
                each(heads, lambda head: arrived(C0, head, 0, y, 0))
                attend(heads, 0, y, None, first=True)

    def o_copy(head):
        columns = pl.ds(pl.multiple_of(head * lanes, lanes), lanes)
        return pltpu.make_async_copy(o_rows.at[head], o_hbm.at[:, columns], o_sem.at[head])

    from_across = (z >= 2) & (y == 0)

    def pass_on_second(head):
        @pl.when(z >= 1)
        def _():
            arrived(Y1, head, 1, 1 - y, c)
            send(C1Y, head, 1, 1 - y, c, twin)

        @pl.when(z >= 2)
        def _():
            arrived(Z2, head, 2, y, c)

            @pl.when(y == 1)
            def _():
                send(Y2, head, 2, y, c, across)

            @pl.when(c == 1)
            def _():
                send(C2, head, 2, y, c, twin)

    def pass_on_last(head):
        arrived(Y2, head, 2, 1, c)
        send(C2Y, head, 2, 1, c, twin)

    @pl.loop(0, steps + 2)
    def _(step):
        @pl.when(step < steps)
        def _():
            pass_on_second(step * HEADS_AT_ONCE)

        @pl.when((step >= 1) & (step <= steps))
        def _():
            heads = (step - 1) * HEADS_AT_ONCE

            @pl.when(z >= 1)
            def _():
                each(heads, lambda head: arrived(C1Y, head, 1, 1 - y, 1 - c))
                attend(heads, 1, 1 - y, None)

            @pl.when((z >= 2) & (c == 0))
            def _():
                each(heads, lambda head: arrived(C2, head, 2, y, 1))
                attend(heads, 2, y, None)

            @pl.when((z >= 2) & (c == 1))
            def _():
                attend(heads, 2, y, 1)

        @pl.when(step < steps)
        def _():
            for at in range(1, HEADS_AT_ONCE):
                pass_on_second(step * HEADS_AT_ONCE + at)

        @pl.when(step >= 2)
        def _():
            heads = (step - 2) * HEADS_AT_ONCE

            @pl.when(from_across)
            def _():
                each(heads, lambda head: arrived(C2Y, head, 2, 1, 1 - c))
                attend(heads, 2, 1, None)

            for at in range(HEADS_AT_ONCE):
                head = heads + at
                result = total[head] * (1.0 / row_sum[head])
                for own in range(GROUP_HEADS):
                    own_cols = slice(own * tokens, (own + 1) * tokens)
                    columns = slice(own * HEAD_WIDTH, (own + 1) * HEAD_WIDTH)
                    o_rows[head, :, columns] = result[:, own_cols].T.astype(jnp.bfloat16)
                o_copy(head).start()

        @pl.when((step >= 1) & (step <= steps) & from_across)
        def _():
            each((step - 1) * HEADS_AT_ONCE, pass_on_last)

    @pl.loop(0, KEY_VALUE_HEADS)
    def _(head):
        o_copy(head).wait()

        def sent(kind, behind, from_y, from_c):
            here = slot(behind, head, from_y, from_c)
            hop(kind, head, here, here, twin).wait_send()

        @pl.when(z < 3)
        def _():
            sent(Z1, 0, y, c)

        @pl.when(y == 0)
        def _():
            sent(Y0, 0, y, c)

        @pl.when(c == 0)
        def _():
            sent(C0, 0, y, c)

        @pl.when(y == 1)
        def _():
            sent(C0Y, 0, 0, c)

        @pl.when(z >= 1)
        def _():
            @pl.when(z < 3)
            def _():
                sent(Z2, 1, y, c)

            sent(Y1, 1, y, c)
            sent(C1, 1, y, c)
            sent(C1Y, 1, 1 - y, c)

        @pl.when((z >= 2) & (y == 1))
        def _():
            sent(Y2, 2, y, c)

        @pl.when((z >= 2) & (c == 1))
        def _():
            sent(C2, 2, y, c)

        @pl.when(from_across)
        def _():
            sent(C2Y, 2, 1, c)


def relay_attention(rotated_queries, key_rows, value_matrix, doc_lengths):
    tokens = rotated_queries.shape[0]
    lanes = GROUP_HEADS * tokens
    in_hbm = pl.BlockSpec(memory_space=pl.ANY)
    pairs = 9 * tokens * tokens * QUERY_HEADS
    return pl.pallas_call(
        relay_kernel,
        out_shape=jax.ShapeDtypeStruct(rotated_queries.shape, jnp.bfloat16),
        in_specs=[in_hbm] * 4,
        out_specs=pl.BlockSpec(memory_space=pl.ANY),
        scratch_shapes=[
            pltpu.SMEM(doc_lengths.shape, jnp.int32),
            pltpu.VMEM((3, KEY_VALUE_HEADS, 2, 2, 2, tokens, HEAD_WIDTH), jnp.bfloat16),
            pltpu.VMEM(rotated_queries.shape, jnp.bfloat16),
            pltpu.VMEM((KEY_VALUE_HEADS, tokens, HEAD_WIDTH), jnp.bfloat16),
            pltpu.VMEM((KEY_VALUE_HEADS, HEAD_WIDTH, lanes), jnp.bfloat16),
            pltpu.VMEM((KEY_VALUE_HEADS, 1, lanes), jnp.float32),
            pltpu.VMEM((KEY_VALUE_HEADS, 1, lanes), jnp.float32),
            pltpu.VMEM((KEY_VALUE_HEADS, HEAD_WIDTH, lanes), jnp.float32),
            pltpu.VMEM((KEY_VALUE_HEADS, tokens, GROUP_HEADS * HEAD_WIDTH), jnp.bfloat16),
            pltpu.SemaphoreType.DMA,
            pltpu.SemaphoreType.DMA((KEY_VALUE_HEADS,)),
            pltpu.SemaphoreType.DMA((KEY_VALUE_HEADS,)),
            pltpu.SemaphoreType.DMA,
            pltpu.SemaphoreType.DMA((KEY_VALUE_HEADS,)),
            pltpu.SemaphoreType.DMA((HOPS, KEY_VALUE_HEADS)),
            pltpu.SemaphoreType.DMA((HOPS, KEY_VALUE_HEADS)),
        ],
        compiler_params=pltpu.CompilerParams(
            collective_id=0, has_side_effects=True, vmem_limit_bytes=64 * 1024 * 1024
        ),
        cost_estimate=pl.CostEstimate(
            flops=4 * pairs * HEAD_WIDTH, bytes_accessed=4 * 1024 * 1024, transcendentals=pairs
        ),
        name="relay_attention",
    )(doc_lengths, rotated_queries, key_rows, value_matrix)


def solution(mesh):
    in_specs = (
        P(("groups", "ctx"), None),
        P(("groups", "ctx"), None),
        P(("groups", "ctx"), None),
        P("groups"),
    )
    out_specs = P(("groups", "ctx"), None)
    body = relay_attention if mesh.shape["ctx"] == 16 else per_device
    return jax.shard_map(
        body, mesh=mesh, in_specs=in_specs, out_specs=out_specs, check_vma=False
    )
```

```python
import math

import jax
import jax.numpy as jnp
from jax import lax
from jax.experimental import pallas as pl
from jax.experimental.pallas import tpu as pltpu
from jax.sharding import PartitionSpec as P

QUERY_HEADS = 16
KEY_VALUE_HEADS = 4
HEAD_WIDTH = 128


masked_score = -1e30


def from_behind(shard, axis, by):
    peers = lax.axis_size(axis)
    pairs = [(i, i + by) for i in range(peers) if 0 <= i + by < peers]
    return lax.ppermute(shard, axis, pairs)


def doc_start_of(query_pos, doc_lengths):
    doc_ends = jnp.cumsum(doc_lengths)
    taken_lengths = jnp.where(doc_ends[None, :] <= query_pos[:, None], doc_lengths[None, :], 0)
    return jnp.sum(taken_lengths, axis=1)


def fold_block(state_now, block_slice, key_start, grouped_heads, query_pos, query_start):
    run_max, run_sum, accumulated = state_now
    token_count = block_slice.shape[1]
    local_keys = block_slice[0].reshape(token_count, KEY_VALUE_HEADS, HEAD_WIDTH)
    local_values = block_slice[1].reshape(token_count, KEY_VALUE_HEADS, HEAD_WIDTH)
    scores = jnp.einsum(
        "tkgd,skd->tkgs", grouped_heads, local_keys, preferred_element_type=jnp.float32
    ) * HEAD_WIDTH ** (-0.5)
    key_pos = key_start + jnp.arange(token_count, dtype=jnp.int32)
    allowed = (key_pos[None, :] >= query_start[:, None]) & (key_pos[None, :] <= query_pos[:, None])
    allowed = allowed[:, None, None, :]
    scores = jnp.where(allowed, scores, masked_score)
    new_max = jnp.maximum(run_max, jnp.max(scores, axis=-1))
    weights = jnp.where(allowed, jnp.exp(scores - new_max[..., None]), 0.0)
    factor = jnp.exp(run_max - new_max)
    run_sum = run_sum * factor + jnp.sum(weights, axis=-1)
    accumulated = accumulated * factor[..., None] + jnp.einsum(
        "tkgs,skd->tkgd",
        weights.astype(jnp.bfloat16),
        local_values,
        preferred_element_type=jnp.float32,
    )
    return (new_max, run_sum, accumulated)


def visit_block(state_now, block_slice, key_start, grouped_heads, query_pos, query_start):
    return fold_block(state_now, block_slice, key_start, grouped_heads, query_pos, query_start)


def per_device(rotated_queries, key_rows, value_matrix, doc_lengths):
    count_of_rows = rotated_queries.shape[0]
    span_count = lax.axis_size("ctx") // 2
    device_index = lax.axis_index("ctx")
    query_pos = device_index * count_of_rows + jnp.arange(count_of_rows, dtype=jnp.int32)
    query_start = doc_start_of(query_pos, doc_lengths)
    grouped_heads = rotated_queries.reshape(
        count_of_rows, KEY_VALUE_HEADS, QUERY_HEADS // KEY_VALUE_HEADS, HEAD_WIDTH
    )
    statistic_shape = (count_of_rows, KEY_VALUE_HEADS, QUERY_HEADS // KEY_VALUE_HEADS)
    state_now = (
        jnp.full(statistic_shape, masked_score, jnp.float32),
        jnp.zeros(statistic_shape, jnp.float32),
        jnp.zeros(statistic_shape + (HEAD_WIDTH,), jnp.float32),
    )
    own_block = jnp.stack([key_rows, value_matrix])
    state_now = visit_block(
        state_now, own_block, device_index * count_of_rows, grouped_heads, query_pos, query_start
    )
    stored = own_block[None]
    for level_number in range(16):
        held_count = stored.shape[0]
        send_count = min(held_count, span_count + 1 - held_count)
        if send_count > 0:
            arrived = from_behind(stored[:send_count], "ctx", held_count)

            def arrived_step(offset_number, inner_state, arrived=arrived, held_count=held_count):
                block_slice = lax.dynamic_index_in_dim(arrived, offset_number, 0, keepdims=False)
                key_start = (device_index - held_count - offset_number) * count_of_rows
                return visit_block(
                    inner_state, block_slice, key_start, grouped_heads, query_pos, query_start
                )

            state_now = lax.fori_loop(0, send_count, arrived_step, state_now)
            stored = jnp.concatenate([stored, arrived], axis=0)
    run_max, run_sum, accumulated = state_now
    result = accumulated / run_sum[..., None]
    return result.reshape(count_of_rows, QUERY_HEADS * HEAD_WIDTH).astype(jnp.bfloat16)


MESH = pl.DeviceIdType.MESH
GROUP_HEADS = QUERY_HEADS // KEY_VALUE_HEADS
EXP2_SCALE = math.log2(math.e) / math.sqrt(HEAD_WIDTH)

(Z1, Z2, C0, C1, C2, YA, YB, CYA, CYB) = range(9)
HOPS = 9
HEADS_AT_ONCE = 2


def relay_kernel(
    lengths_hbm, q_hbm, k_hbm, v_hbm, o_hbm,
    lengths, held, q_rows, v_rows, q_cols, row_max, row_sum, total, o_rows,
    lengths_sem, k_sem, v_sem, q_sem, o_sem, send_sem, recv_sem,
):
    tokens = q_hbm.shape[0]
    lanes = GROUP_HEADS * tokens
    group = lax.axis_index("groups")
    me = lax.axis_index("ctx")
    z, y, c = me // 4, (me // 2) % 2, me % 2
    up, down = me + 4, me - 4
    across = me + 2 - 4 * y
    twin = me + 1 - 2 * c

    def place(device):
        return (group, device)

    def slot(behind, head, from_y, from_c):
        return held.at[behind, head, from_y, :, from_c]

    def k_copy(head):
        columns = pl.ds(head * HEAD_WIDTH, HEAD_WIDTH)
        return pltpu.make_async_copy(k_hbm.at[:, columns], held.at[0, head, y, 0, c], k_sem.at[head])

    def v_copy(head):
        columns = pl.ds(head * HEAD_WIDTH, HEAD_WIDTH)
        return pltpu.make_async_copy(v_hbm.at[:, columns], v_rows.at[head], v_sem.at[head])

    def hop(kind, head, source, target, device):
        return pltpu.make_async_remote_copy(
            src_ref=source, dst_ref=target, send_sem=send_sem.at[kind, head],
            recv_sem=recv_sem.at[kind, head], device_id=place(device), device_id_type=MESH,
        )

    def send(kind, head, behind, from_y, from_c, device, landing=None):
        landing = behind if landing is None else landing
        hop(kind, head, slot(behind, head, from_y, from_c), slot(landing, head, from_y, from_c), device).start()

    def arrived(kind, head, behind, from_y, from_c):
        here = slot(behind, head, from_y, from_c)
        hop(kind, head, here, here, twin).wait_recv()

    q_copy = pltpu.make_async_copy(q_hbm, q_rows, q_sem)
    lengths_copy = pltpu.make_async_copy(lengths_hbm, lengths, lengths_sem)
    for head in range(KEY_VALUE_HEADS):
        v_copy(head).start()
        k_copy(head).start()
    q_copy.start()
    lengths_copy.start()

    barrier = pltpu.get_barrier_semaphore()

    def greet(device):
        pl.semaphore_signal(barrier, inc=1, device_id=place(device), device_id_type=MESH)

    greet(twin)
    greet(across)

    @pl.when(z < 3)
    def _():
        greet(up)

    @pl.when(z > 0)
    def _():
        greet(down)

    for head in range(KEY_VALUE_HEADS):
        v_copy(head).wait()
        held[0, head, y, 1, c] = v_rows[head].astype(jnp.float32).T.astype(jnp.bfloat16)

    inner = (z > 0) & (z < 3)

    @pl.when(inner)
    def _():
        pl.semaphore_wait(barrier, 4)

    @pl.when(jnp.logical_not(inner))
    def _():
        pl.semaphore_wait(barrier, 3)

    for head in range(KEY_VALUE_HEADS):
        k_copy(head).wait()

        @pl.when(z < 3)
        def _():
            send(Z1, head, 0, y, c, up, landing=1)

        @pl.when(y == 0)
        def _():
            send(YA, head, 0, y, c, across)

        @pl.when(c == 0)
        def _():
            send(C0, head, 0, y, c, twin)

    lengths_copy.wait()
    q_copy.wait()
    for head in range(QUERY_HEADS):
        rows = q_rows[:, head * HEAD_WIDTH:(head + 1) * HEAD_WIDTH].astype(jnp.float32)
        at = head % GROUP_HEADS
        q_cols[head // GROUP_HEADS, :, at * tokens:(at + 1) * tokens] = rows.T.astype(jnp.bfloat16)

    query_pos = me * tokens + lax.broadcasted_iota(jnp.int32, (1, lanes), 1) % tokens
    doc_end = jnp.int32(0)
    query_start = jnp.zeros((1, lanes), jnp.int32)
    for doc in range(lengths.shape[0]):
        doc_end = doc_end + lengths[doc]
        query_start = query_start + jnp.where(doc_end <= query_pos, lengths[doc], 0)

    half = lanes // 2
    chains = [(at, part) for at in range(HEADS_AT_ONCE) for part in range(2)]

    def attend(heads, behind, from_y, from_c, first=False):
        count = tokens if from_c is not None else 2 * tokens
        key_start = ((z - behind) * 4 + from_y * 2 + (0 if from_c is None else from_c)) * tokens
        key_pos = lax.broadcasted_iota(jnp.int32, (count, half), 0)

        def cols_of(part):
            return slice(part * half, (part + 1) * half)

        def scores_of(chain):
            at, part = chain
            if from_c is None:
                keys = held[behind, heads + at, from_y, 0].reshape(count, HEAD_WIDTH)
            else:
                keys = held[behind, heads + at, from_y, 0, from_c]
            return jnp.dot(keys, q_cols[heads + at, :, cols_of(part)], preferred_element_type=jnp.float32)

        def fold(chain, scores):
            at, part = chain
            head, cols = heads + at, cols_of(part)
            if from_c is None:
                values = jnp.concatenate(
                    [held[behind, head, from_y, 1, 0], held[behind, head, from_y, 1, 1]], axis=1
                )
            else:
                values = held[behind, head, from_y, 1, from_c]
            allowed = key_pos >= query_start[:, cols] - key_start
            if first:
                allowed = allowed & (key_pos <= query_pos[:, cols] - key_start)
            scores = jnp.where(allowed, scores, masked_score)
            new_max = jnp.max(scores, axis=0, keepdims=True)
            if not first:
                old_max = row_max[head, :, cols]
                new_max = jnp.maximum(old_max, new_max)
            weights = jnp.exp2((scores - new_max) * EXP2_SCALE)
            weight_sum = jnp.sum(weights, axis=0, keepdims=True)
            mixed = jnp.dot(values, weights.astype(jnp.bfloat16), preferred_element_type=jnp.float32)
            if first:
                row_sum[head, :, cols] = weight_sum
                total[head, :, cols] = mixed
            else:
                factor = jnp.exp2((old_max - new_max) * EXP2_SCALE)
                row_sum[head, :, cols] = row_sum[head, :, cols] * factor + weight_sum
                total[head, :, cols] = total[head, :, cols] * factor + mixed
            row_max[head, :, cols] = new_max

        ready = scores_of(chains[0])
        for number, chain in enumerate(chains):
            scores = ready
            if number + 1 < len(chains):
                ready = scores_of(chains[number + 1])
            fold(chain, scores)

    def each(heads, wait):
        for at in range(HEADS_AT_ONCE):
            wait(heads + at)

    def z_first(head):
        @pl.when(z >= 1)
        def _():
            arrived(Z1, head, 1, y, c)

            @pl.when(z < 3)
            def _():
                send(Z2, head, 1, y, c, up, landing=2)

            send(YB - y, head, 1, y, c, across)
            send(C1, head, 1, y, c, twin)

    def z_second(head):
        @pl.when(z >= 2)
        def _():
            arrived(Z2, head, 2, y, c)

            @pl.when(y == 1)
            def _():
                send(YB, head, 2, y, c, across)

            @pl.when(c == 1)
            def _():
                send(C2, head, 2, y, c, twin)

    crosses_first, crosses_second = z + y >= 1, z + y >= 2

    def y_first(head):
        @pl.when(crosses_first)
        def _():
            arrived(YA, head, 1 - y, 1 - y, c)
            send(CYA, head, 1 - y, 1 - y, c, twin)

    def y_second(head):
        @pl.when(crosses_second)
        def _():
            arrived(YB, head, 2 - y, 1 - y, c)
            send(CYB, head, 2 - y, 1 - y, c, twin)

    def o_copy(head):
        columns = pl.ds(pl.multiple_of(head * lanes, lanes), lanes)
        return pltpu.make_async_copy(o_rows.at[head], o_hbm.at[:, columns], o_sem.at[head])

    @pl.loop(0, 2)
    def _(step):
        heads = step * HEADS_AT_ONCE

        @pl.when(c == 0)
        def _():
            attend(heads, 0, y, 0, first=True)

        @pl.when(c == 1)
        def _():
            each(heads, lambda head: arrived(C0, head, 0, y, 0))
            attend(heads, 0, y, None, first=True)

        z_first(step)

    y_first(0)

    @pl.loop(0, 2)
    def _(step):
        heads = step * HEADS_AT_ONCE

        @pl.when(step == 0)
        def _():
            z_first(2)
            y_first(1)

        @pl.when(step == 1)
        def _():
            y_first(3)

        @pl.when(z >= 1)
        def _():
            each(heads, lambda head: arrived(C1, head, 1, y, 1 - c))
            attend(heads, 1, y, None)

        @pl.when(step == 0)
        def _():
            z_first(3)
            y_first(2)

        @pl.when(step == 1)
        def _():
            z_second(0)

        @pl.when(crosses_first)
        def _():
            each(heads, lambda head: arrived(CYA, head, 1 - y, 1 - y, 1 - c))
            attend(heads, 1 - y, 1 - y, None)

    z_second(1)
    y_second(0)
    z_second(2)
    y_second(1)

    @pl.loop(0, 2)
    def _(step):
        heads = step * HEADS_AT_ONCE

        @pl.when((z >= 2) & (c == 0))
        def _():
            each(heads, lambda head: arrived(C2, head, 2, y, 1))
            attend(heads, 2, y, None)

        @pl.when((z >= 2) & (c == 1))
        def _():
            attend(heads, 2, y, 1)

        @pl.when(step == 0)
        def _():
            z_second(3)
            y_second(2)

        @pl.when(step == 1)
        def _():
            y_second(3)

        @pl.when(crosses_second)
        def _():
            each(heads, lambda head: arrived(CYB, head, 2 - y, 1 - y, 1 - c))
            attend(heads, 2 - y, 1 - y, None)

        for at in range(HEADS_AT_ONCE):
            head = heads + at
            result = total[head] * (1.0 / row_sum[head])
            for own in range(GROUP_HEADS):
                own_cols = slice(own * tokens, (own + 1) * tokens)
                columns = slice(own * HEAD_WIDTH, (own + 1) * HEAD_WIDTH)
                o_rows[head, :, columns] = result[:, own_cols].T.astype(jnp.bfloat16)
            o_copy(head).start()

    @pl.loop(0, KEY_VALUE_HEADS)
    def _(head):
        o_copy(head).wait()

        def sent(kind, behind, from_y, from_c):
            here = slot(behind, head, from_y, from_c)
            hop(kind, head, here, here, twin).wait_send()

        @pl.when(z < 3)
        def _():
            sent(Z1, 0, y, c)

        @pl.when(c == 0)
        def _():
            sent(C0, 0, y, c)

        @pl.when(z - y >= 0)
        def _():
            sent(YA, y, y, c)

        @pl.when(z - y >= 1)
        def _():
            sent(YB, 1 + y, y, c)

        @pl.when(crosses_first)
        def _():
            sent(CYA, 1 - y, 1 - y, c)

        @pl.when(crosses_second)
        def _():
            sent(CYB, 2 - y, 1 - y, c)

        @pl.when(z >= 1)
        def _():
            sent(C1, 1, y, c)

            @pl.when(z < 3)
            def _():
                sent(Z2, 1, y, c)

        @pl.when((z >= 2) & (c == 1))
        def _():
            sent(C2, 2, y, c)


def relay_attention(rotated_queries, key_rows, value_matrix, doc_lengths):
    tokens = rotated_queries.shape[0]
    lanes = GROUP_HEADS * tokens
    in_hbm = pl.BlockSpec(memory_space=pl.ANY)
    pairs = 9 * tokens * tokens * QUERY_HEADS
    return pl.pallas_call(
        relay_kernel,
        out_shape=jax.ShapeDtypeStruct(rotated_queries.shape, jnp.bfloat16),
        in_specs=[in_hbm] * 4,
        out_specs=pl.BlockSpec(memory_space=pl.ANY),
        scratch_shapes=[
            pltpu.SMEM(doc_lengths.shape, jnp.int32),
            pltpu.VMEM((3, KEY_VALUE_HEADS, 2, 2, 2, tokens, HEAD_WIDTH), jnp.bfloat16),
            pltpu.VMEM(rotated_queries.shape, jnp.bfloat16),
            pltpu.VMEM((KEY_VALUE_HEADS, tokens, HEAD_WIDTH), jnp.bfloat16),
            pltpu.VMEM((KEY_VALUE_HEADS, HEAD_WIDTH, lanes), jnp.bfloat16),
            pltpu.VMEM((KEY_VALUE_HEADS, 1, lanes), jnp.float32),
            pltpu.VMEM((KEY_VALUE_HEADS, 1, lanes), jnp.float32),
            pltpu.VMEM((KEY_VALUE_HEADS, HEAD_WIDTH, lanes), jnp.float32),
            pltpu.VMEM((KEY_VALUE_HEADS, tokens, GROUP_HEADS * HEAD_WIDTH), jnp.bfloat16),
            pltpu.SemaphoreType.DMA,
            pltpu.SemaphoreType.DMA((KEY_VALUE_HEADS,)),
            pltpu.SemaphoreType.DMA((KEY_VALUE_HEADS,)),
            pltpu.SemaphoreType.DMA,
            pltpu.SemaphoreType.DMA((KEY_VALUE_HEADS,)),
            pltpu.SemaphoreType.DMA((HOPS, KEY_VALUE_HEADS)),
            pltpu.SemaphoreType.DMA((HOPS, KEY_VALUE_HEADS)),
        ],
        compiler_params=pltpu.CompilerParams(
            collective_id=0, has_side_effects=True, vmem_limit_bytes=64 * 1024 * 1024
        ),
        cost_estimate=pl.CostEstimate(
            flops=4 * pairs * HEAD_WIDTH, bytes_accessed=4 * 1024 * 1024, transcendentals=pairs
        ),
        name="relay_attention",
    )(doc_lengths, rotated_queries, key_rows, value_matrix)


def solution(mesh):
    in_specs = (
        P(("groups", "ctx"), None),
        P(("groups", "ctx"), None),
        P(("groups", "ctx"), None),
        P("groups"),
    )
    out_specs = P(("groups", "ctx"), None)
    body = relay_attention if mesh.shape["ctx"] == 16 else per_device
    return jax.shard_map(
        body, mesh=mesh, in_specs=in_specs, out_specs=out_specs, check_vma=False
    )
```

```python
import math

import jax
import jax.numpy as jnp
from jax import lax
from jax.experimental import pallas as pl
from jax.experimental.pallas import tpu as pltpu
from jax.sharding import PartitionSpec as P

QUERY_HEADS = 16
KEY_VALUE_HEADS = 4
HEAD_WIDTH = 128


masked_score = -1e30


def from_behind(shard, axis, by):
    peers = lax.axis_size(axis)
    pairs = [(i, i + by) for i in range(peers) if 0 <= i + by < peers]
    return lax.ppermute(shard, axis, pairs)


def doc_start_of(query_pos, doc_lengths):
    doc_ends = jnp.cumsum(doc_lengths)
    taken_lengths = jnp.where(doc_ends[None, :] <= query_pos[:, None], doc_lengths[None, :], 0)
    return jnp.sum(taken_lengths, axis=1)


def fold_block(state_now, block_slice, key_start, grouped_heads, query_pos, query_start):
    run_max, run_sum, accumulated = state_now
    token_count = block_slice.shape[1]
    local_keys = block_slice[0].reshape(token_count, KEY_VALUE_HEADS, HEAD_WIDTH)
    local_values = block_slice[1].reshape(token_count, KEY_VALUE_HEADS, HEAD_WIDTH)
    scores = jnp.einsum(
        "tkgd,skd->tkgs", grouped_heads, local_keys, preferred_element_type=jnp.float32
    ) * HEAD_WIDTH ** (-0.5)
    key_pos = key_start + jnp.arange(token_count, dtype=jnp.int32)
    allowed = (key_pos[None, :] >= query_start[:, None]) & (key_pos[None, :] <= query_pos[:, None])
    allowed = allowed[:, None, None, :]
    scores = jnp.where(allowed, scores, masked_score)
    new_max = jnp.maximum(run_max, jnp.max(scores, axis=-1))
    weights = jnp.where(allowed, jnp.exp(scores - new_max[..., None]), 0.0)
    factor = jnp.exp(run_max - new_max)
    run_sum = run_sum * factor + jnp.sum(weights, axis=-1)
    accumulated = accumulated * factor[..., None] + jnp.einsum(
        "tkgs,skd->tkgd",
        weights.astype(jnp.bfloat16),
        local_values,
        preferred_element_type=jnp.float32,
    )
    return (new_max, run_sum, accumulated)


def visit_block(state_now, block_slice, key_start, grouped_heads, query_pos, query_start):
    return fold_block(state_now, block_slice, key_start, grouped_heads, query_pos, query_start)


def per_device(rotated_queries, key_rows, value_matrix, doc_lengths):
    count_of_rows = rotated_queries.shape[0]
    span_count = lax.axis_size("ctx") // 2
    device_index = lax.axis_index("ctx")
    query_pos = device_index * count_of_rows + jnp.arange(count_of_rows, dtype=jnp.int32)
    query_start = doc_start_of(query_pos, doc_lengths)
    grouped_heads = rotated_queries.reshape(
        count_of_rows, KEY_VALUE_HEADS, QUERY_HEADS // KEY_VALUE_HEADS, HEAD_WIDTH
    )
    statistic_shape = (count_of_rows, KEY_VALUE_HEADS, QUERY_HEADS // KEY_VALUE_HEADS)
    state_now = (
        jnp.full(statistic_shape, masked_score, jnp.float32),
        jnp.zeros(statistic_shape, jnp.float32),
        jnp.zeros(statistic_shape + (HEAD_WIDTH,), jnp.float32),
    )
    own_block = jnp.stack([key_rows, value_matrix])
    state_now = visit_block(
        state_now, own_block, device_index * count_of_rows, grouped_heads, query_pos, query_start
    )
    stored = own_block[None]
    for level_number in range(16):
        held_count = stored.shape[0]
        send_count = min(held_count, span_count + 1 - held_count)
        if send_count > 0:
            arrived = from_behind(stored[:send_count], "ctx", held_count)

            def arrived_step(offset_number, inner_state, arrived=arrived, held_count=held_count):
                block_slice = lax.dynamic_index_in_dim(arrived, offset_number, 0, keepdims=False)
                key_start = (device_index - held_count - offset_number) * count_of_rows
                return visit_block(
                    inner_state, block_slice, key_start, grouped_heads, query_pos, query_start
                )

            state_now = lax.fori_loop(0, send_count, arrived_step, state_now)
            stored = jnp.concatenate([stored, arrived], axis=0)
    run_max, run_sum, accumulated = state_now
    result = accumulated / run_sum[..., None]
    return result.reshape(count_of_rows, QUERY_HEADS * HEAD_WIDTH).astype(jnp.bfloat16)


MESH = pl.DeviceIdType.MESH
GROUP_HEADS = QUERY_HEADS // KEY_VALUE_HEADS
EXP2_SCALE = math.log2(math.e) / math.sqrt(HEAD_WIDTH)

(Z1, Z2, C0, C1, C2, YA, YB, CYA, CYB) = range(9)
HOPS = 9
HEADS_AT_ONCE = 2


def relay_kernel(
    lengths_hbm, q_hbm, k_hbm, v_hbm, o_hbm,
    lengths, held, q_rows, v_rows, q_cols, row_max, row_sum, total, o_rows,
    lengths_sem, k_sem, v_sem, q_sem, o_sem, send_sem, recv_sem,
):
    tokens = q_hbm.shape[0]
    lanes = GROUP_HEADS * tokens
    group = lax.axis_index("groups")
    me = lax.axis_index("ctx")
    z, y, c = me // 4, (me // 2) % 2, me % 2
    up, down = me + 4, me - 4
    across = me + 2 - 4 * y
    twin = me + 1 - 2 * c

    def place(device):
        return (group, device)

    def slot(behind, head, from_y, from_c):
        return held.at[behind, head, from_y, :, from_c]

    def k_copy(head):
        columns = pl.ds(head * HEAD_WIDTH, HEAD_WIDTH)
        return pltpu.make_async_copy(k_hbm.at[:, columns], held.at[0, head, y, 0, c], k_sem.at[head])

    def v_copy(head):
        columns = pl.ds(head * HEAD_WIDTH, HEAD_WIDTH)
        return pltpu.make_async_copy(v_hbm.at[:, columns], v_rows.at[head], v_sem.at[head])

    def hop(kind, head, source, target, device):
        return pltpu.make_async_remote_copy(
            src_ref=source, dst_ref=target, send_sem=send_sem.at[kind, head],
            recv_sem=recv_sem.at[kind, head], device_id=place(device), device_id_type=MESH,
        )

    def send(kind, head, behind, from_y, from_c, device, landing=None):
        landing = behind if landing is None else landing
        hop(kind, head, slot(behind, head, from_y, from_c), slot(landing, head, from_y, from_c), device).start()

    def arrived(kind, head, behind, from_y, from_c):
        here = slot(behind, head, from_y, from_c)
        hop(kind, head, here, here, twin).wait_recv()

    q_copy = pltpu.make_async_copy(q_hbm, q_rows, q_sem)
    lengths_copy = pltpu.make_async_copy(lengths_hbm, lengths, lengths_sem)
    for head in range(KEY_VALUE_HEADS):
        v_copy(head).start()
        k_copy(head).start()
    q_copy.start()
    lengths_copy.start()

    barrier = pltpu.get_barrier_semaphore()

    def greet(device):
        pl.semaphore_signal(barrier, inc=1, device_id=place(device), device_id_type=MESH)

    greet(twin)
    greet(across)

    @pl.when(z < 3)
    def _():
        greet(up)

    @pl.when(z > 0)
    def _():
        greet(down)

    for head in range(KEY_VALUE_HEADS):
        v_copy(head).wait()
        held[0, head, y, 1, c] = v_rows[head].astype(jnp.float32).T.astype(jnp.bfloat16)

    inner = (z > 0) & (z < 3)

    @pl.when(inner)
    def _():
        pl.semaphore_wait(barrier, 4)

    @pl.when(jnp.logical_not(inner))
    def _():
        pl.semaphore_wait(barrier, 3)

    for head in range(KEY_VALUE_HEADS):
        k_copy(head).wait()

        @pl.when(z < 3)
        def _():
            send(Z1, head, 0, y, c, up, landing=1)

        @pl.when(y == 0)
        def _():
            send(YA, head, 0, y, c, across)

        @pl.when(c == 0)
        def _():
            send(C0, head, 0, y, c, twin)

    lengths_copy.wait()
    q_copy.wait()
    for head in range(QUERY_HEADS):
        rows = q_rows[:, head * HEAD_WIDTH:(head + 1) * HEAD_WIDTH].astype(jnp.float32)
        at = head % GROUP_HEADS
        q_cols[head // GROUP_HEADS, :, at * tokens:(at + 1) * tokens] = rows.T.astype(jnp.bfloat16)

    query_pos = me * tokens + lax.broadcasted_iota(jnp.int32, (1, lanes), 1) % tokens
    doc_end = jnp.int32(0)
    query_start = jnp.zeros((1, lanes), jnp.int32)
    for doc in range(lengths.shape[0]):
        doc_end = doc_end + lengths[doc]
        query_start = query_start + jnp.where(doc_end <= query_pos, lengths[doc], 0)

    half = lanes // 2
    chains = [(at, part) for at in range(HEADS_AT_ONCE) for part in range(2)]

    def attend(heads, behind, from_y, from_c, first=False):
        count = tokens if from_c is not None else 2 * tokens
        key_start = ((z - behind) * 4 + from_y * 2 + (0 if from_c is None else from_c)) * tokens
        key_pos = lax.broadcasted_iota(jnp.int32, (count, half), 0)

        def cols_of(part):
            return slice(part * half, (part + 1) * half)

        def scores_of(chain):
            at, part = chain
            if from_c is None:
                keys = held[behind, heads + at, from_y, 0].reshape(count, HEAD_WIDTH)
            else:
                keys = held[behind, heads + at, from_y, 0, from_c]
            return jnp.dot(keys, q_cols[heads + at, :, cols_of(part)], preferred_element_type=jnp.float32)

        def top_of(chain, scores):
            at, part = chain
            cols = cols_of(part)
            allowed = key_pos >= query_start[:, cols] - key_start
            if first:
                allowed = allowed & (key_pos <= query_pos[:, cols] - key_start)
            scores = jnp.where(allowed, scores, masked_score)
            best, rows = scores, count
            while rows > 8:
                rows //= 2
                best = jnp.maximum(best[:rows], best[rows:])
            return scores, jnp.max(best, axis=0, keepdims=True)

        def values_of(chain):
            head = heads + chain[0]
            if from_c is None:
                values = jnp.concatenate(
                    [held[behind, head, from_y, 1, 0], held[behind, head, from_y, 1, 1]], axis=1
                )
            else:
                values = held[behind, head, from_y, 1, from_c]
            return jnp.concatenate([values, jnp.ones((16, count), jnp.bfloat16)], axis=0)

        masked = [top_of(chain, scores_of(chain)) for chain in chains]
        highest, olds = [], []
        for (at, part), (scores, top) in zip(chains, masked):
            old_max = None if first else row_max[heads + at, :, cols_of(part)]
            olds.append(old_max)
            highest.append(top if first else jnp.maximum(old_max, top))
        weights = [
            jnp.exp2((scores - new_max) * EXP2_SCALE).astype(jnp.bfloat16)
            for (scores, _), new_max in zip(masked, highest)
        ]
        mixed = [
            jnp.dot(values_of(chain), weight, preferred_element_type=jnp.float32)
            for chain, weight in zip(chains, weights)
        ]
        for (at, part), old_max, new_max, mix in zip(chains, olds, highest, mixed):
            head, cols = heads + at, cols_of(part)
            if first:
                row_sum[head, :, cols] = mix[HEAD_WIDTH:HEAD_WIDTH + 1]
                total[head, :, cols] = mix[:HEAD_WIDTH]
            else:
                factor = jnp.exp2((old_max - new_max) * EXP2_SCALE)
                row_sum[head, :, cols] = row_sum[head, :, cols] * factor + mix[HEAD_WIDTH:HEAD_WIDTH + 1]
                total[head, :, cols] = total[head, :, cols] * factor + mix[:HEAD_WIDTH]
            row_max[head, :, cols] = new_max

    def each(heads, wait):
        for at in range(HEADS_AT_ONCE):
            wait(heads + at)

    def z_first(head):
        @pl.when(z >= 1)
        def _():
            arrived(Z1, head, 1, y, c)

            @pl.when(z < 3)
            def _():
                send(Z2, head, 1, y, c, up, landing=2)

            send(YB - y, head, 1, y, c, across)
            send(C1, head, 1, y, c, twin)

    def z_second(head):
        @pl.when(z >= 2)
        def _():
            arrived(Z2, head, 2, y, c)

            @pl.when(y == 1)
            def _():
                send(YB, head, 2, y, c, across)

            @pl.when(c == 1)
            def _():
                send(C2, head, 2, y, c, twin)

    crosses_first, crosses_second = z + y >= 1, z + y >= 2

    def y_first(head):
        @pl.when(crosses_first)
        def _():
            arrived(YA, head, 1 - y, 1 - y, c)
            send(CYA, head, 1 - y, 1 - y, c, twin)

    def y_second(head):
        @pl.when(crosses_second)
        def _():
            arrived(YB, head, 2 - y, 1 - y, c)
            send(CYB, head, 2 - y, 1 - y, c, twin)

    def o_copy(head):
        columns = pl.ds(pl.multiple_of(head * lanes, lanes), lanes)
        return pltpu.make_async_copy(o_rows.at[head], o_hbm.at[:, columns], o_sem.at[head])

    @pl.loop(0, 2)
    def _(step):
        heads = step * HEADS_AT_ONCE

        @pl.when(c == 0)
        def _():
            attend(heads, 0, y, 0, first=True)

        @pl.when(c == 1)
        def _():
            each(heads, lambda head: arrived(C0, head, 0, y, 0))
            attend(heads, 0, y, None, first=True)

        z_first(step)

    y_first(0)

    @pl.loop(0, 2)
    def _(step):
        heads = step * HEADS_AT_ONCE

        @pl.when(step == 0)
        def _():
            z_first(2)
            y_first(1)

        @pl.when(step == 1)
        def _():
            y_first(3)

        @pl.when(z >= 1)
        def _():
            each(heads, lambda head: arrived(C1, head, 1, y, 1 - c))
            attend(heads, 1, y, None)

        @pl.when(step == 0)
        def _():
            z_first(3)
            y_first(2)

        @pl.when(step == 1)
        def _():
            z_second(0)

        @pl.when(crosses_first)
        def _():
            each(heads, lambda head: arrived(CYA, head, 1 - y, 1 - y, 1 - c))
            attend(heads, 1 - y, 1 - y, None)

    z_second(1)
    y_second(0)
    z_second(2)
    y_second(1)

    @pl.loop(0, 2)
    def _(step):
        heads = step * HEADS_AT_ONCE

        @pl.when((z >= 2) & (c == 0))
        def _():
            each(heads, lambda head: arrived(C2, head, 2, y, 1))
            attend(heads, 2, y, None)

        @pl.when((z >= 2) & (c == 1))
        def _():
            attend(heads, 2, y, 1)

        @pl.when(step == 0)
        def _():
            z_second(3)
            y_second(2)

        @pl.when(step == 1)
        def _():
            y_second(3)

        @pl.when(crosses_second)
        def _():
            each(heads, lambda head: arrived(CYB, head, 2 - y, 1 - y, 1 - c))
            attend(heads, 2 - y, 1 - y, None)

        for at in range(HEADS_AT_ONCE):
            head = heads + at
            result = total[head] * (1.0 / row_sum[head])
            for own in range(GROUP_HEADS):
                own_cols = slice(own * tokens, (own + 1) * tokens)
                columns = slice(own * HEAD_WIDTH, (own + 1) * HEAD_WIDTH)
                o_rows[head, :, columns] = result[:, own_cols].astype(jnp.bfloat16).T
            o_copy(head).start()

    @pl.loop(0, KEY_VALUE_HEADS)
    def _(head):
        o_copy(head).wait()

        def sent(kind, behind, from_y, from_c):
            here = slot(behind, head, from_y, from_c)
            hop(kind, head, here, here, twin).wait_send()

        @pl.when(z < 3)
        def _():
            sent(Z1, 0, y, c)

        @pl.when(c == 0)
        def _():
            sent(C0, 0, y, c)

        @pl.when(z - y >= 0)
        def _():
            sent(YA, y, y, c)

        @pl.when(z - y >= 1)
        def _():
            sent(YB, 1 + y, y, c)

        @pl.when(crosses_first)
        def _():
            sent(CYA, 1 - y, 1 - y, c)

        @pl.when(crosses_second)
        def _():
            sent(CYB, 2 - y, 1 - y, c)

        @pl.when(z >= 1)
        def _():
            sent(C1, 1, y, c)

            @pl.when(z < 3)
            def _():
                sent(Z2, 1, y, c)

        @pl.when((z >= 2) & (c == 1))
        def _():
            sent(C2, 2, y, c)


def relay_attention(rotated_queries, key_rows, value_matrix, doc_lengths):
    tokens = rotated_queries.shape[0]
    lanes = GROUP_HEADS * tokens
    in_hbm = pl.BlockSpec(memory_space=pl.ANY)
    pairs = 9 * tokens * tokens * QUERY_HEADS
    return pl.pallas_call(
        relay_kernel,
        out_shape=pltpu.VMEM(rotated_queries.shape, jnp.bfloat16),
        in_specs=[in_hbm] * 4,
        out_specs=pl.BlockSpec(memory_space=pl.ANY),
        scratch_shapes=[
            pltpu.SMEM(doc_lengths.shape, jnp.int32),
            pltpu.VMEM((3, KEY_VALUE_HEADS, 2, 2, 2, tokens, HEAD_WIDTH), jnp.bfloat16),
            pltpu.VMEM(rotated_queries.shape, jnp.bfloat16),
            pltpu.VMEM((KEY_VALUE_HEADS, tokens, HEAD_WIDTH), jnp.bfloat16),
            pltpu.VMEM((KEY_VALUE_HEADS, HEAD_WIDTH, lanes), jnp.bfloat16),
            pltpu.VMEM((KEY_VALUE_HEADS, 1, lanes), jnp.float32),
            pltpu.VMEM((KEY_VALUE_HEADS, 1, lanes), jnp.float32),
            pltpu.VMEM((KEY_VALUE_HEADS, HEAD_WIDTH, lanes), jnp.float32),
            pltpu.VMEM((KEY_VALUE_HEADS, tokens, GROUP_HEADS * HEAD_WIDTH), jnp.bfloat16),
            pltpu.SemaphoreType.DMA,
            pltpu.SemaphoreType.DMA((KEY_VALUE_HEADS,)),
            pltpu.SemaphoreType.DMA((KEY_VALUE_HEADS,)),
            pltpu.SemaphoreType.DMA,
            pltpu.SemaphoreType.DMA((KEY_VALUE_HEADS,)),
            pltpu.SemaphoreType.DMA((HOPS, KEY_VALUE_HEADS)),
            pltpu.SemaphoreType.DMA((HOPS, KEY_VALUE_HEADS)),
        ],
        compiler_params=pltpu.CompilerParams(
            collective_id=0, has_side_effects=True, vmem_limit_bytes=60 * 1024 * 1024
        ),
        cost_estimate=pl.CostEstimate(
            flops=4 * pairs * HEAD_WIDTH, bytes_accessed=4 * 1024 * 1024, transcendentals=pairs
        ),
        name="relay_attention",
    )(doc_lengths, rotated_queries, key_rows, value_matrix)


def solution(mesh):
    in_specs = (
        P(("groups", "ctx"), None),
        P(("groups", "ctx"), None),
        P(("groups", "ctx"), None),
        P("groups"),
    )
    out_specs = P(("groups", "ctx"), None)
    body = relay_attention if mesh.shape["ctx"] == 16 else per_device
    return jax.shard_map(
        body, mesh=mesh, in_specs=in_specs, out_specs=out_specs, check_vma=False
    )
```

```python
import math

import jax
import jax.numpy as jnp
from jax import lax
from jax.experimental import pallas as pl
from jax.experimental.pallas import tpu as pltpu
from jax.sharding import PartitionSpec as P

QUERY_HEADS = 16
KEY_VALUE_HEADS = 4
HEAD_WIDTH = 128


masked_score = -1e30


def from_behind(shard, axis, by):
    peers = lax.axis_size(axis)
    pairs = [(i, i + by) for i in range(peers) if 0 <= i + by < peers]
    return lax.ppermute(shard, axis, pairs)


def doc_start_of(query_pos, doc_lengths):
    doc_ends = jnp.cumsum(doc_lengths)
    taken_lengths = jnp.where(doc_ends[None, :] <= query_pos[:, None], doc_lengths[None, :], 0)
    return jnp.sum(taken_lengths, axis=1)


def fold_block(state_now, block_slice, key_start, grouped_heads, query_pos, query_start):
    run_max, run_sum, accumulated = state_now
    token_count = block_slice.shape[1]
    local_keys = block_slice[0].reshape(token_count, KEY_VALUE_HEADS, HEAD_WIDTH)
    local_values = block_slice[1].reshape(token_count, KEY_VALUE_HEADS, HEAD_WIDTH)
    scores = jnp.einsum(
        "tkgd,skd->tkgs", grouped_heads, local_keys, preferred_element_type=jnp.float32
    ) * HEAD_WIDTH ** (-0.5)
    key_pos = key_start + jnp.arange(token_count, dtype=jnp.int32)
    allowed = (key_pos[None, :] >= query_start[:, None]) & (key_pos[None, :] <= query_pos[:, None])
    allowed = allowed[:, None, None, :]
    scores = jnp.where(allowed, scores, masked_score)
    new_max = jnp.maximum(run_max, jnp.max(scores, axis=-1))
    weights = jnp.where(allowed, jnp.exp(scores - new_max[..., None]), 0.0)
    factor = jnp.exp(run_max - new_max)
    run_sum = run_sum * factor + jnp.sum(weights, axis=-1)
    accumulated = accumulated * factor[..., None] + jnp.einsum(
        "tkgs,skd->tkgd",
        weights.astype(jnp.bfloat16),
        local_values,
        preferred_element_type=jnp.float32,
    )
    return (new_max, run_sum, accumulated)


def visit_block(state_now, block_slice, key_start, grouped_heads, query_pos, query_start):
    return fold_block(state_now, block_slice, key_start, grouped_heads, query_pos, query_start)


def per_device(rotated_queries, key_rows, value_matrix, doc_lengths):
    count_of_rows = rotated_queries.shape[0]
    span_count = lax.axis_size("ctx") // 2
    device_index = lax.axis_index("ctx")
    query_pos = device_index * count_of_rows + jnp.arange(count_of_rows, dtype=jnp.int32)
    query_start = doc_start_of(query_pos, doc_lengths)
    grouped_heads = rotated_queries.reshape(
        count_of_rows, KEY_VALUE_HEADS, QUERY_HEADS // KEY_VALUE_HEADS, HEAD_WIDTH
    )
    statistic_shape = (count_of_rows, KEY_VALUE_HEADS, QUERY_HEADS // KEY_VALUE_HEADS)
    state_now = (
        jnp.full(statistic_shape, masked_score, jnp.float32),
        jnp.zeros(statistic_shape, jnp.float32),
        jnp.zeros(statistic_shape + (HEAD_WIDTH,), jnp.float32),
    )
    own_block = jnp.stack([key_rows, value_matrix])
    state_now = visit_block(
        state_now, own_block, device_index * count_of_rows, grouped_heads, query_pos, query_start
    )
    stored = own_block[None]
    for level_number in range(16):
        held_count = stored.shape[0]
        send_count = min(held_count, span_count + 1 - held_count)
        if send_count > 0:
            arrived = from_behind(stored[:send_count], "ctx", held_count)

            def arrived_step(offset_number, inner_state, arrived=arrived, held_count=held_count):
                block_slice = lax.dynamic_index_in_dim(arrived, offset_number, 0, keepdims=False)
                key_start = (device_index - held_count - offset_number) * count_of_rows
                return visit_block(
                    inner_state, block_slice, key_start, grouped_heads, query_pos, query_start
                )

            state_now = lax.fori_loop(0, send_count, arrived_step, state_now)
            stored = jnp.concatenate([stored, arrived], axis=0)
    run_max, run_sum, accumulated = state_now
    result = accumulated / run_sum[..., None]
    return result.reshape(count_of_rows, QUERY_HEADS * HEAD_WIDTH).astype(jnp.bfloat16)


MESH = pl.DeviceIdType.MESH
GROUP_HEADS = QUERY_HEADS // KEY_VALUE_HEADS
EXP2_SCALE = math.log2(math.e) / math.sqrt(HEAD_WIDTH)

(Z1, Z2, YA, YB, C0, C1, CYA, C2, CYB) = range(9)
HOPS = 9
HEADS_AT_ONCE = 2


def relay_kernel(
    lengths_hbm, q_hbm, k_hbm, v_hbm, o_hbm,
    lengths, held, q_rows, v_rows, q_cols, row_max, row_sum, total, o_rows,
    lengths_sem, k_sem, v_sem, q_sem, o_sem, send_sem, recv_sem,
):
    tokens = q_hbm.shape[0]
    lanes = GROUP_HEADS * tokens
    group = lax.axis_index("groups")
    me = lax.axis_index("ctx")
    z, y, c = me // 4, (me // 2) % 2, me % 2
    up, down = me + 4, me - 4
    across = me + 2 - 4 * y
    twin = me + 1 - 2 * c

    def place(device):
        return (group, device)

    def slot(behind, head, from_y, from_c):
        return held.at[behind, head, from_y, :, from_c]

    def k_copy(head):
        columns = pl.ds(head * HEAD_WIDTH, HEAD_WIDTH)
        return pltpu.make_async_copy(k_hbm.at[:, columns], held.at[0, head, y, 0, c], k_sem.at[head])

    def v_copy(head):
        columns = pl.ds(head * HEAD_WIDTH, HEAD_WIDTH)
        return pltpu.make_async_copy(v_hbm.at[:, columns], v_rows.at[head], v_sem.at[head])

    def hop(kind, head, source, target, device):
        return pltpu.make_async_remote_copy(
            src_ref=source, dst_ref=target, send_sem=send_sem.at[kind, head],
            recv_sem=recv_sem.at[kind, head], device_id=place(device), device_id_type=MESH,
        )

    def send(kind, head, behind, from_y, from_c, device, landing=None):
        landing = behind if landing is None else landing
        hop(kind, head, slot(behind, head, from_y, from_c), slot(landing, head, from_y, from_c), device).start()

    def arrived(kind, head, behind, from_y, from_c):
        here = slot(behind, head, from_y, from_c)
        hop(kind, head, here, here, twin).wait_recv()

    q_copy = pltpu.make_async_copy(q_hbm, q_rows, q_sem)
    lengths_copy = pltpu.make_async_copy(lengths_hbm, lengths, lengths_sem)
    for head in range(KEY_VALUE_HEADS):
        v_copy(head).start()
        k_copy(head).start()
    q_copy.start()
    lengths_copy.start()

    barrier = pltpu.get_barrier_semaphore()

    def greet(device):
        pl.semaphore_signal(barrier, inc=1, device_id=place(device), device_id_type=MESH)

    greet(twin)
    greet(across)

    @pl.when(z < 3)
    def _():
        greet(up)

    @pl.when(z > 0)
    def _():
        greet(down)

    row_max[...] = jnp.full(row_max.shape, masked_score, jnp.float32)
    row_sum[...] = jnp.zeros(row_sum.shape, jnp.float32)
    total[...] = jnp.zeros(total.shape, jnp.float32)
    for head in range(KEY_VALUE_HEADS):
        blank = jnp.zeros((2, tokens, HEAD_WIDTH), jnp.bfloat16)

        @pl.when(c == 0)
        def _():
            held[0, head, y, :, 1] = blank

        @pl.when(c == 1)
        def _():
            held[2, head, y, :, 0] = blank

    for head in range(KEY_VALUE_HEADS):
        v_copy(head).wait()
        held[0, head, y, 1, c] = v_rows[head].astype(jnp.float32).T.astype(jnp.bfloat16)

    inner = (z > 0) & (z < 3)

    @pl.when(inner)
    def _():
        pl.semaphore_wait(barrier, 4)

    @pl.when(jnp.logical_not(inner))
    def _():
        pl.semaphore_wait(barrier, 3)

    for head in range(KEY_VALUE_HEADS):
        k_copy(head).wait()

        @pl.when(z < 3)
        def _():
            send(Z1, head, 0, y, c, up, landing=1)

        @pl.when(y == 0)
        def _():
            send(YA, head, 0, y, c, across)

        @pl.when(c == 0)
        def _():
            send(C0, head, 0, y, c, twin)

    lengths_copy.wait()
    q_copy.wait()
    for head in range(QUERY_HEADS):
        rows = q_rows[:, head * HEAD_WIDTH:(head + 1) * HEAD_WIDTH].astype(jnp.float32)
        at = head % GROUP_HEADS
        q_cols[head // GROUP_HEADS, :, at * tokens:(at + 1) * tokens] = rows.T.astype(jnp.bfloat16)

    query_pos = me * tokens + lax.broadcasted_iota(jnp.int32, (1, lanes), 1) % tokens
    doc_end = jnp.int32(0)
    query_start = jnp.zeros((1, lanes), jnp.int32)
    for doc in range(lengths.shape[0]):
        doc_end = doc_end + lengths[doc]
        query_start = query_start + jnp.where(doc_end <= query_pos, lengths[doc], 0)

    half = lanes // 2
    chains = [(at, part) for at in range(HEADS_AT_ONCE) for part in range(2)]

    def attend(heads, behind, from_y):
        count = 2 * tokens
        key_start = ((z - behind) * 4 + from_y * 2) * tokens
        key_pos = lax.broadcasted_iota(jnp.int32, (count, half), 0)

        def cols_of(part):
            return slice(part * half, (part + 1) * half)

        def scores_of(chain):
            at, part = chain
            keys = held[behind, heads + at, from_y, 0].reshape(count, HEAD_WIDTH)
            return jnp.dot(keys, q_cols[heads + at, :, cols_of(part)], preferred_element_type=jnp.float32)

        def top_of(chain, scores):
            at, part = chain
            cols = cols_of(part)
            allowed = (key_pos >= query_start[:, cols] - key_start) & (key_pos <= query_pos[:, cols] - key_start)
            scores = jnp.where(allowed, scores, masked_score)
            best, rows = scores, count
            while rows > 8:
                rows //= 2
                best = jnp.maximum(best[:rows], best[rows:])
            return scores, jnp.max(best, axis=0, keepdims=True)

        def values_of(chain):
            head = heads + chain[0]
            values = jnp.concatenate(
                [held[behind, head, from_y, 1, 0], held[behind, head, from_y, 1, 1]], axis=1
            )
            return jnp.concatenate([values, jnp.ones((16, count), jnp.bfloat16)], axis=0)

        masked = [top_of(chain, scores_of(chain)) for chain in chains]
        highest, olds = [], []
        for (at, part), (scores, top) in zip(chains, masked):
            old_max = row_max[heads + at, :, cols_of(part)]
            olds.append(old_max)
            highest.append(jnp.maximum(old_max, top))
        weights = [
            jnp.exp2((scores - new_max) * EXP2_SCALE).astype(jnp.bfloat16)
            for (scores, _), new_max in zip(masked, highest)
        ]
        mixed = [
            jnp.dot(values_of(chain), weight, preferred_element_type=jnp.float32)
            for chain, weight in zip(chains, weights)
        ]
        for (at, part), old_max, new_max, mix in zip(chains, olds, highest, mixed):
            head, cols = heads + at, cols_of(part)
            factor = jnp.exp2((old_max - new_max) * EXP2_SCALE)
            row_sum[head, :, cols] = row_sum[head, :, cols] * factor + mix[HEAD_WIDTH:HEAD_WIDTH + 1]
            total[head, :, cols] = total[head, :, cols] * factor + mix[:HEAD_WIDTH]
            row_max[head, :, cols] = new_max

    def each(heads, wait):
        for at in range(HEADS_AT_ONCE):
            wait(heads + at)

    def z_first(head):
        @pl.when(z >= 1)
        def _():
            arrived(Z1, head, 1, y, c)

            @pl.when(z < 3)
            def _():
                send(Z2, head, 1, y, c, up, landing=2)

            send(YB - y, head, 1, y, c, across)
            send(C1, head, 1, y, c, twin)

    def z_second(head):
        @pl.when(z >= 2)
        def _():
            arrived(Z2, head, 2, y, c)

            @pl.when(y == 1)
            def _():
                send(YB, head, 2, y, c, across)

            @pl.when(c == 1)
            def _():
                send(C2, head, 2, y, c, twin)

    crosses_first, crosses_second = z + y >= 1, z + y >= 2

    def y_first(head):
        @pl.when(crosses_first)
        def _():
            arrived(YA, head, 1 - y, 1 - y, c)
            send(CYA, head, 1 - y, 1 - y, c, twin)

    def y_second(head):
        @pl.when(crosses_second)
        def _():
            arrived(YB, head, 2 - y, 1 - y, c)
            send(CYB, head, 2 - y, 1 - y, c, twin)

    def o_copy(head):
        columns = pl.ds(pl.multiple_of(head * lanes, lanes), lanes)
        return pltpu.make_async_copy(o_rows.at[head], o_hbm.at[:, columns], o_sem.at[head])

    ahead = {
        1: [(z_first, 0)],
        2: [(z_first, 1), (y_first, 0), (z_first, 2), (y_first, 1)],
        3: [(z_first, 3), (y_first, 2)],
        4: [(y_first, 3)],
        5: [(z_second, 0)],
        6: [(z_second, 1), (y_second, 0), (z_second, 2), (y_second, 1)],
        7: [(z_second, 3), (y_second, 2)],
        9: [(y_second, 3)],
    }

    @pl.loop(0, 10)
    def _(item):
        later = (item + 8) // 10
        kind = later * (1 + (item + 8) % 2 + 2 * ((item + 8) // 14))
        pair = (1 - later) * item + later * (((item + 8) // 2 + 1) % 2)
        heads = pair * HEADS_AT_ONCE
        crossed = (1 - kind % 2) * ((kind + 4) // 5)
        behind = (kind + 1) // 2 - crossed * y
        from_y = y + crossed * (1 - 2 * y)

        for number, steps in ahead.items():
            @pl.when(item == number)
            def _():
                for pass_on, head in steps:
                    pass_on(head)

        @pl.when(z >= behind)
        def _():
            @pl.when(((kind != 0) | (c == 1)) & ((kind != 3) | (c == 0)))
            def _():
                each(heads, lambda head: arrived(C0 + kind, head, behind, from_y, 1 - c))

            attend(heads, behind, from_y)

        @pl.when((item == 7) | (item == 9))
        def _():
            for at in range(HEADS_AT_ONCE):
                head = heads + at
                result = total[head] * (1.0 / row_sum[head])
                for own in range(GROUP_HEADS):
                    own_cols = slice(own * tokens, (own + 1) * tokens)
                    columns = slice(own * HEAD_WIDTH, (own + 1) * HEAD_WIDTH)
                    o_rows[head, :, columns] = result[:, own_cols].astype(jnp.bfloat16).T
                o_copy(head).start()

    @pl.loop(0, KEY_VALUE_HEADS)
    def _(head):
        o_copy(head).wait()

        def sent(kind, behind, from_y, from_c):
            here = slot(behind, head, from_y, from_c)
            hop(kind, head, here, here, twin).wait_send()

        @pl.when(z < 3)
        def _():
            sent(Z1, 0, y, c)

        @pl.when(c == 0)
        def _():
            sent(C0, 0, y, c)

        @pl.when(z - y >= 0)
        def _():
            sent(YA, y, y, c)

        @pl.when(z - y >= 1)
        def _():
            sent(YB, 1 + y, y, c)

        @pl.when(crosses_first)
        def _():
            sent(CYA, 1 - y, 1 - y, c)

        @pl.when(crosses_second)
        def _():
            sent(CYB, 2 - y, 1 - y, c)

        @pl.when(z >= 1)
        def _():
            sent(C1, 1, y, c)

            @pl.when(z < 3)
            def _():
                sent(Z2, 1, y, c)

        @pl.when((z >= 2) & (c == 1))
        def _():
            sent(C2, 2, y, c)


def relay_attention(rotated_queries, key_rows, value_matrix, doc_lengths):
    tokens = rotated_queries.shape[0]
    lanes = GROUP_HEADS * tokens
    in_hbm = pl.BlockSpec(memory_space=pl.ANY)
    pairs = 9 * tokens * tokens * QUERY_HEADS
    return pl.pallas_call(
        relay_kernel,
        out_shape=pltpu.VMEM(rotated_queries.shape, jnp.bfloat16),
        in_specs=[in_hbm] * 4,
        out_specs=pl.BlockSpec(memory_space=pl.ANY),
        scratch_shapes=[
            pltpu.SMEM(doc_lengths.shape, jnp.int32),
            pltpu.VMEM((3, KEY_VALUE_HEADS, 2, 2, 2, tokens, HEAD_WIDTH), jnp.bfloat16),
            pltpu.VMEM(rotated_queries.shape, jnp.bfloat16),
            pltpu.VMEM((KEY_VALUE_HEADS, tokens, HEAD_WIDTH), jnp.bfloat16),
            pltpu.VMEM((KEY_VALUE_HEADS, HEAD_WIDTH, lanes), jnp.bfloat16),
            pltpu.VMEM((KEY_VALUE_HEADS, 1, lanes), jnp.float32),
            pltpu.VMEM((KEY_VALUE_HEADS, 1, lanes), jnp.float32),
            pltpu.VMEM((KEY_VALUE_HEADS, HEAD_WIDTH, lanes), jnp.float32),
            pltpu.VMEM((KEY_VALUE_HEADS, tokens, GROUP_HEADS * HEAD_WIDTH), jnp.bfloat16),
            pltpu.SemaphoreType.DMA,
            pltpu.SemaphoreType.DMA((KEY_VALUE_HEADS,)),
            pltpu.SemaphoreType.DMA((KEY_VALUE_HEADS,)),
            pltpu.SemaphoreType.DMA,
            pltpu.SemaphoreType.DMA((KEY_VALUE_HEADS,)),
            pltpu.SemaphoreType.DMA((HOPS, KEY_VALUE_HEADS)),
            pltpu.SemaphoreType.DMA((HOPS, KEY_VALUE_HEADS)),
        ],
        compiler_params=pltpu.CompilerParams(
            collective_id=0, has_side_effects=True, vmem_limit_bytes=60 * 1024 * 1024
        ),
        cost_estimate=pl.CostEstimate(
            flops=4 * pairs * HEAD_WIDTH, bytes_accessed=4 * 1024 * 1024, transcendentals=pairs
        ),
        name="relay_attention",
    )(doc_lengths, rotated_queries, key_rows, value_matrix)


def solution(mesh):
    in_specs = (
        P(("groups", "ctx"), None),
        P(("groups", "ctx"), None),
        P(("groups", "ctx"), None),
        P("groups"),
    )
    out_specs = P(("groups", "ctx"), None)
    body = relay_attention if mesh.shape["ctx"] == 16 else per_device
    return jax.shard_map(
        body, mesh=mesh, in_specs=in_specs, out_specs=out_specs, check_vma=False
    )
```

```python
import math

import jax
import jax.numpy as jnp
from jax import lax
from jax.experimental import pallas as pl
from jax.experimental.pallas import tpu as pltpu
from jax.sharding import PartitionSpec as P

QUERY_HEADS = 16
KEY_VALUE_HEADS = 4
HEAD_WIDTH = 128


masked_score = -1e30


def from_behind(shard, axis, by):
    peers = lax.axis_size(axis)
    pairs = [(i, i + by) for i in range(peers) if 0 <= i + by < peers]
    return lax.ppermute(shard, axis, pairs)


def doc_start_of(query_pos, doc_lengths):
    doc_ends = jnp.cumsum(doc_lengths)
    taken_lengths = jnp.where(doc_ends[None, :] <= query_pos[:, None], doc_lengths[None, :], 0)
    return jnp.sum(taken_lengths, axis=1)


def fold_block(state_now, block_slice, key_start, grouped_heads, query_pos, query_start):
    run_max, run_sum, accumulated = state_now
    token_count = block_slice.shape[1]
    local_keys = block_slice[0].reshape(token_count, KEY_VALUE_HEADS, HEAD_WIDTH)
    local_values = block_slice[1].reshape(token_count, KEY_VALUE_HEADS, HEAD_WIDTH)
    scores = jnp.einsum(
        "tkgd,skd->tkgs", grouped_heads, local_keys, preferred_element_type=jnp.float32
    ) * HEAD_WIDTH ** (-0.5)
    key_pos = key_start + jnp.arange(token_count, dtype=jnp.int32)
    allowed = (key_pos[None, :] >= query_start[:, None]) & (key_pos[None, :] <= query_pos[:, None])
    allowed = allowed[:, None, None, :]
    scores = jnp.where(allowed, scores, masked_score)
    new_max = jnp.maximum(run_max, jnp.max(scores, axis=-1))
    weights = jnp.where(allowed, jnp.exp(scores - new_max[..., None]), 0.0)
    factor = jnp.exp(run_max - new_max)
    run_sum = run_sum * factor + jnp.sum(weights, axis=-1)
    accumulated = accumulated * factor[..., None] + jnp.einsum(
        "tkgs,skd->tkgd",
        weights.astype(jnp.bfloat16),
        local_values,
        preferred_element_type=jnp.float32,
    )
    return (new_max, run_sum, accumulated)


def visit_block(state_now, block_slice, key_start, grouped_heads, query_pos, query_start):
    return fold_block(state_now, block_slice, key_start, grouped_heads, query_pos, query_start)


def per_device(rotated_queries, key_rows, value_matrix, doc_lengths):
    count_of_rows = rotated_queries.shape[0]
    span_count = lax.axis_size("ctx") // 2
    device_index = lax.axis_index("ctx")
    query_pos = device_index * count_of_rows + jnp.arange(count_of_rows, dtype=jnp.int32)
    query_start = doc_start_of(query_pos, doc_lengths)
    grouped_heads = rotated_queries.reshape(
        count_of_rows, KEY_VALUE_HEADS, QUERY_HEADS // KEY_VALUE_HEADS, HEAD_WIDTH
    )
    statistic_shape = (count_of_rows, KEY_VALUE_HEADS, QUERY_HEADS // KEY_VALUE_HEADS)
    state_now = (
        jnp.full(statistic_shape, masked_score, jnp.float32),
        jnp.zeros(statistic_shape, jnp.float32),
        jnp.zeros(statistic_shape + (HEAD_WIDTH,), jnp.float32),
    )
    own_block = jnp.stack([key_rows, value_matrix])
    state_now = visit_block(
        state_now, own_block, device_index * count_of_rows, grouped_heads, query_pos, query_start
    )
    stored = own_block[None]
    for level_number in range(16):
        held_count = stored.shape[0]
        send_count = min(held_count, span_count + 1 - held_count)
        if send_count > 0:
            arrived = from_behind(stored[:send_count], "ctx", held_count)

            def arrived_step(offset_number, inner_state, arrived=arrived, held_count=held_count):
                block_slice = lax.dynamic_index_in_dim(arrived, offset_number, 0, keepdims=False)
                key_start = (device_index - held_count - offset_number) * count_of_rows
                return visit_block(
                    inner_state, block_slice, key_start, grouped_heads, query_pos, query_start
                )

            state_now = lax.fori_loop(0, send_count, arrived_step, state_now)
            stored = jnp.concatenate([stored, arrived], axis=0)
    run_max, run_sum, accumulated = state_now
    result = accumulated / run_sum[..., None]
    return result.reshape(count_of_rows, QUERY_HEADS * HEAD_WIDTH).astype(jnp.bfloat16)


MESH = pl.DeviceIdType.MESH
GROUP_HEADS = QUERY_HEADS // KEY_VALUE_HEADS
EXP2_SCALE = math.log2(math.e) / math.sqrt(HEAD_WIDTH)

(Z1, Z2, C0, C1, C2, YA, YB, CYA, CYB, ZY) = range(10)
HOPS = 10
HEADS_AT_ONCE = 2


def relay_kernel(
    lengths_hbm, q_hbm, k_hbm, v_hbm, o_hbm,
    lengths, held, q_rows, v_rows, q_cols, row_max, row_sum, total, o_rows,
    lengths_sem, k_sem, v_sem, q_sem, o_sem, send_sem, recv_sem,
):
    tokens = q_hbm.shape[0]
    lanes = GROUP_HEADS * tokens
    group = lax.axis_index("groups")
    me = lax.axis_index("ctx")
    z, y, c = me // 4, (me // 2) % 2, me % 2
    up, down = me + 4, me - 4
    across = me + 2 - 4 * y
    twin = me + 1 - 2 * c

    def place(device):
        return (group, device)

    def slot(behind, head, from_y, from_c):
        return held.at[behind, head, from_y, :, from_c]

    def k_copy(head):
        columns = pl.ds(head * HEAD_WIDTH, HEAD_WIDTH)
        return pltpu.make_async_copy(k_hbm.at[:, columns], held.at[0, head, y, 0, c], k_sem.at[head])

    def v_copy(head):
        columns = pl.ds(head * HEAD_WIDTH, HEAD_WIDTH)
        return pltpu.make_async_copy(v_hbm.at[:, columns], v_rows.at[head], v_sem.at[head])

    def hop(kind, head, source, target, device, landing_kind=None):
        return pltpu.make_async_remote_copy(
            src_ref=source, dst_ref=target, send_sem=send_sem.at[kind, head],
            recv_sem=recv_sem.at[kind if landing_kind is None else landing_kind, head], device_id=place(device), device_id_type=MESH,
        )

    def send(kind, head, behind, from_y, from_c, device, landing=None):
        landing = behind if landing is None else landing
        hop(kind, head, slot(behind, head, from_y, from_c), slot(landing, head, from_y, from_c), device).start()

    def arrived(kind, head, behind, from_y, from_c):
        here = slot(behind, head, from_y, from_c)
        hop(kind, head, here, here, twin).wait_recv()

    q_copy = pltpu.make_async_copy(q_hbm, q_rows, q_sem)
    lengths_copy = pltpu.make_async_copy(lengths_hbm, lengths, lengths_sem)
    for head in range(KEY_VALUE_HEADS):
        v_copy(head).start()
        k_copy(head).start()
    q_copy.start()
    lengths_copy.start()

    barrier = pltpu.get_barrier_semaphore()

    def greet(device):
        pl.semaphore_signal(barrier, inc=1, device_id=place(device), device_id_type=MESH)

    greet(twin)
    greet(across)

    @pl.when(z < 3)
    def _():
        greet(up)

    @pl.when(z > 0)
    def _():
        greet(down)

    for head in range(KEY_VALUE_HEADS):
        v_copy(head).wait()
        held[0, head, y, 1, c] = v_rows[head].astype(jnp.float32).T.astype(jnp.bfloat16)

    inner = (z > 0) & (z < 3)

    @pl.when(inner)
    def _():
        pl.semaphore_wait(barrier, 4)

    @pl.when(jnp.logical_not(inner))
    def _():
        pl.semaphore_wait(barrier, 3)

    for head in range(KEY_VALUE_HEADS):
        k_copy(head).wait()

        @pl.when(z < 3)
        def _():
            send(Z1, head, 0, y, c, up, landing=1)

        @pl.when(y == 0)
        def _():
            send(YA, head, 0, y, c, across)

        @pl.when(c == 0)
        def _():
            send(C0, head, 0, y, c, twin)

    lengths_copy.wait()
    q_copy.wait()
    for head in range(QUERY_HEADS):
        rows = q_rows[:, head * HEAD_WIDTH:(head + 1) * HEAD_WIDTH].astype(jnp.float32)
        at = head % GROUP_HEADS
        q_cols[head // GROUP_HEADS, :, at * tokens:(at + 1) * tokens] = rows.T.astype(jnp.bfloat16)

    query_pos = me * tokens + lax.broadcasted_iota(jnp.int32, (1, lanes), 1) % tokens
    doc_end = jnp.int32(0)
    query_start = jnp.zeros((1, lanes), jnp.int32)
    for doc in range(lengths.shape[0]):
        doc_end = doc_end + lengths[doc]
        query_start = query_start + jnp.where(doc_end <= query_pos, lengths[doc], 0)

    half = lanes // 2
    chains = [(at, part) for at in range(HEADS_AT_ONCE) for part in range(2)]

    def attend(heads, behind, from_y, from_c, first=False):
        count = tokens if from_c is not None else 2 * tokens
        key_start = ((z - behind) * 4 + from_y * 2 + (0 if from_c is None else from_c)) * tokens
        key_pos = lax.broadcasted_iota(jnp.int32, (count, half), 0)

        def cols_of(part):
            return slice(part * half, (part + 1) * half)

        def scores_of(chain):
            at, part = chain
            if from_c is None:
                keys = held[behind, heads + at, from_y, 0].reshape(count, HEAD_WIDTH)
            else:
                keys = held[behind, heads + at, from_y, 0, from_c]
            return jnp.dot(keys, q_cols[heads + at, :, cols_of(part)], preferred_element_type=jnp.float32)

        def top_of(chain, scores):
            at, part = chain
            cols = cols_of(part)
            allowed = key_pos >= query_start[:, cols] - key_start
            if first:
                allowed = allowed & (key_pos <= query_pos[:, cols] - key_start)
            scores = jnp.where(allowed, scores, masked_score)
            best, rows = scores, count
            while rows > 8:
                rows //= 2
                best = jnp.maximum(best[:rows], best[rows:])
            return scores, jnp.max(best, axis=0, keepdims=True)

        def values_of(chain):
            head = heads + chain[0]
            if from_c is None:
                values = jnp.concatenate(
                    [held[behind, head, from_y, 1, 0], held[behind, head, from_y, 1, 1]], axis=1
                )
            else:
                values = held[behind, head, from_y, 1, from_c]
            return jnp.concatenate([values, jnp.ones((16, count), jnp.bfloat16)], axis=0)

        masked = [top_of(chain, scores_of(chain)) for chain in chains]
        highest, olds = [], []
        for (at, part), (scores, top) in zip(chains, masked):
            old_max = None if first else row_max[heads + at, :, cols_of(part)]
            olds.append(old_max)
            highest.append(top if first else jnp.maximum(old_max, top))
        weights = [
            jnp.exp2((scores - new_max) * EXP2_SCALE).astype(jnp.bfloat16)
            for (scores, _), new_max in zip(masked, highest)
        ]
        mixed = [
            jnp.dot(values_of(chain), weight, preferred_element_type=jnp.float32)
            for chain, weight in zip(chains, weights)
        ]
        for (at, part), old_max, new_max, mix in zip(chains, olds, highest, mixed):
            head, cols = heads + at, cols_of(part)
            if first:
                row_sum[head, :, cols] = mix[HEAD_WIDTH:HEAD_WIDTH + 1]
                total[head, :, cols] = mix[:HEAD_WIDTH]
            else:
                factor = jnp.exp2((old_max - new_max) * EXP2_SCALE)
                row_sum[head, :, cols] = row_sum[head, :, cols] * factor + mix[HEAD_WIDTH:HEAD_WIDTH + 1]
                total[head, :, cols] = total[head, :, cols] * factor + mix[:HEAD_WIDTH]
            row_max[head, :, cols] = new_max

    def each(heads, wait):
        for at in range(HEADS_AT_ONCE):
            wait(heads + at)

    def z_first(head):
        @pl.when(z >= 1)
        def _():
            arrived(Z1, head, 1, y, c)

            @pl.when(z < 3)
            def _():
                send(Z2, head, 1, y, c, up, landing=2)

            send(YB - y, head, 1, y, c, across)
            send(C1, head, 1, y, c, twin)

    def z_second(head):
        @pl.when(z >= 2)
        def _():
            arrived(Z2, head, 2, y, c)

            if head < KEY_VALUE_HEADS - 1:
                @pl.when(y == 1)
                def _():
                    send(YB, head, 2, y, c, across)

            @pl.when(c == 1)
            def _():
                send(C2, head, 2, y, c, twin)

    sends_last = (y == 0) & (z >= 1) & (z < 3)
    crosses_first, crosses_second = z + y >= 1, z + y >= 2

    def y_first(head):
        @pl.when(crosses_first)
        def _():
            arrived(YA, head, 1 - y, 1 - y, c)
            if head == KEY_VALUE_HEADS - 1:
                @pl.when(sends_last)
                def _():
                    hop(ZY, head, slot(1, head, 1, c), slot(2, head, 1, c), up, landing_kind=YB).start()

            send(CYA, head, 1 - y, 1 - y, c, twin)

    def y_second(head):
        @pl.when(crosses_second)
        def _():
            arrived(YB, head, 2 - y, 1 - y, c)
            send(CYB, head, 2 - y, 1 - y, c, twin)

    def o_copy(head):
        columns = pl.ds(pl.multiple_of(head * lanes, lanes), lanes)
        return pltpu.make_async_copy(o_rows.at[head], o_hbm.at[:, columns], o_sem.at[head])

    @pl.loop(0, 2)
    def _(step):
        heads = step * HEADS_AT_ONCE

        @pl.when(c == 0)
        def _():
            attend(heads, 0, y, 0, first=True)

        @pl.when(c == 1)
        def _():
            each(heads, lambda head: arrived(C0, head, 0, y, 0))
            attend(heads, 0, y, None, first=True)

        z_first(step)

    y_first(0)

    @pl.loop(0, 2)
    def _(step):
        heads = step * HEADS_AT_ONCE

        @pl.when(step == 0)
        def _():
            z_first(2)
            y_first(1)

        @pl.when(step == 1)
        def _():
            y_first(3)

        @pl.when(z >= 1)
        def _():
            each(heads, lambda head: arrived(C1, head, 1, y, 1 - c))
            attend(heads, 1, y, None)

        @pl.when(step == 0)
        def _():
            z_first(3)
            y_first(2)

        @pl.when(step == 1)
        def _():
            z_second(0)

        @pl.when(crosses_first)
        def _():
            each(heads, lambda head: arrived(CYA, head, 1 - y, 1 - y, 1 - c))
            attend(heads, 1 - y, 1 - y, None)

    z_second(1)
    y_second(0)

    @pl.loop(0, 2)
    def _(step):
        heads = step * HEADS_AT_ONCE

        @pl.when(step == 1)
        def _():
            z_second(3)
            y_second(2)

        @pl.when((z >= 2) & (c == 0))
        def _():
            each(heads, lambda head: arrived(C2, head, 2, y, 1))
            attend(heads, 2, y, None)

        @pl.when((z >= 2) & (c == 1))
        def _():
            attend(heads, 2, y, 1)

        @pl.when(step == 0)
        def _():
            z_second(2)
            y_second(1)

        @pl.when(step == 1)
        def _():
            y_second(3)

        @pl.when(crosses_second)
        def _():
            each(heads, lambda head: arrived(CYB, head, 2 - y, 1 - y, 1 - c))
            attend(heads, 2 - y, 1 - y, None)

        for at in range(HEADS_AT_ONCE):
            head = heads + at
            result = total[head] * (1.0 / row_sum[head])
            for own in range(GROUP_HEADS):
                own_cols = slice(own * tokens, (own + 1) * tokens)
                columns = slice(own * HEAD_WIDTH, (own + 1) * HEAD_WIDTH)
                o_rows[head, :, columns] = result[:, own_cols].astype(jnp.bfloat16).T
            o_copy(head).start()

    @pl.loop(0, KEY_VALUE_HEADS)
    def _(head):
        o_copy(head).wait()

        def sent(kind, behind, from_y, from_c):
            here = slot(behind, head, from_y, from_c)
            hop(kind, head, here, here, twin).wait_send()

        @pl.when(z < 3)
        def _():
            sent(Z1, 0, y, c)

        @pl.when(c == 0)
        def _():
            sent(C0, 0, y, c)

        @pl.when(z - y >= 0)
        def _():
            sent(YA, y, y, c)

        @pl.when((z - y >= 1) & ((y == 0) | (head < KEY_VALUE_HEADS - 1)))
        def _():
            sent(YB, 1 + y, y, c)

        @pl.when(sends_last & (head == KEY_VALUE_HEADS - 1))
        def _():
            sent(ZY, 1, 1, c)

        @pl.when(crosses_first)
        def _():
            sent(CYA, 1 - y, 1 - y, c)

        @pl.when(crosses_second)
        def _():
            sent(CYB, 2 - y, 1 - y, c)

        @pl.when(z >= 1)
        def _():
            sent(C1, 1, y, c)

            @pl.when(z < 3)
            def _():
                sent(Z2, 1, y, c)

        @pl.when((z >= 2) & (c == 1))
        def _():
            sent(C2, 2, y, c)


def relay_attention(rotated_queries, key_rows, value_matrix, doc_lengths):
    tokens = rotated_queries.shape[0]
    lanes = GROUP_HEADS * tokens
    in_hbm = pl.BlockSpec(memory_space=pl.ANY)
    pairs = 9 * tokens * tokens * QUERY_HEADS
    return pl.pallas_call(
        relay_kernel,
        out_shape=pltpu.VMEM(rotated_queries.shape, jnp.bfloat16),
        in_specs=[in_hbm] * 4,
        out_specs=pl.BlockSpec(memory_space=pl.ANY),
        scratch_shapes=[
            pltpu.SMEM(doc_lengths.shape, jnp.int32),
            pltpu.VMEM((3, KEY_VALUE_HEADS, 2, 2, 2, tokens, HEAD_WIDTH), jnp.bfloat16),
            pltpu.VMEM(rotated_queries.shape, jnp.bfloat16),
            pltpu.VMEM((KEY_VALUE_HEADS, tokens, HEAD_WIDTH), jnp.bfloat16),
            pltpu.VMEM((KEY_VALUE_HEADS, HEAD_WIDTH, lanes), jnp.bfloat16),
            pltpu.VMEM((KEY_VALUE_HEADS, 1, lanes), jnp.float32),
            pltpu.VMEM((KEY_VALUE_HEADS, 1, lanes), jnp.float32),
            pltpu.VMEM((KEY_VALUE_HEADS, HEAD_WIDTH, lanes), jnp.float32),
            pltpu.VMEM((KEY_VALUE_HEADS, tokens, GROUP_HEADS * HEAD_WIDTH), jnp.bfloat16),
            pltpu.SemaphoreType.DMA,
            pltpu.SemaphoreType.DMA((KEY_VALUE_HEADS,)),
            pltpu.SemaphoreType.DMA((KEY_VALUE_HEADS,)),
            pltpu.SemaphoreType.DMA,
            pltpu.SemaphoreType.DMA((KEY_VALUE_HEADS,)),
            pltpu.SemaphoreType.DMA((HOPS, KEY_VALUE_HEADS)),
            pltpu.SemaphoreType.DMA((HOPS, KEY_VALUE_HEADS)),
        ],
        compiler_params=pltpu.CompilerParams(
            collective_id=0, has_side_effects=True, vmem_limit_bytes=60 * 1024 * 1024
        ),
        cost_estimate=pl.CostEstimate(
            flops=4 * pairs * HEAD_WIDTH, bytes_accessed=4 * 1024 * 1024, transcendentals=pairs
        ),
        name="relay_attention",
    )(doc_lengths, rotated_queries, key_rows, value_matrix)


def solution(mesh):
    in_specs = (
        P(("groups", "ctx"), None),
        P(("groups", "ctx"), None),
        P(("groups", "ctx"), None),
        P("groups"),
    )
    out_specs = P(("groups", "ctx"), None)
    body = relay_attention if mesh.shape["ctx"] == 16 else per_device
    return jax.shard_map(
        body, mesh=mesh, in_specs=in_specs, out_specs=out_specs, check_vma=False
    )
```

```python
import math

import jax
import jax.numpy as jnp
from jax import lax
from jax.experimental import pallas as pl
from jax.experimental.pallas import tpu as pltpu
from jax.sharding import PartitionSpec as P

QUERY_HEADS = 16
KEY_VALUE_HEADS = 4
HEAD_WIDTH = 128


masked_score = -1e30


def from_behind(shard, axis, by):
    peers = lax.axis_size(axis)
    pairs = [(i, i + by) for i in range(peers) if 0 <= i + by < peers]
    return lax.ppermute(shard, axis, pairs)


def doc_start_of(query_pos, doc_lengths):
    doc_ends = jnp.cumsum(doc_lengths)
    taken_lengths = jnp.where(doc_ends[None, :] <= query_pos[:, None], doc_lengths[None, :], 0)
    return jnp.sum(taken_lengths, axis=1)


def fold_block(state_now, block_slice, key_start, grouped_heads, query_pos, query_start):
    run_max, run_sum, accumulated = state_now
    token_count = block_slice.shape[1]
    local_keys = block_slice[0].reshape(token_count, KEY_VALUE_HEADS, HEAD_WIDTH)
    local_values = block_slice[1].reshape(token_count, KEY_VALUE_HEADS, HEAD_WIDTH)
    scores = jnp.einsum(
        "tkgd,skd->tkgs", grouped_heads, local_keys, preferred_element_type=jnp.float32
    ) * HEAD_WIDTH ** (-0.5)
    key_pos = key_start + jnp.arange(token_count, dtype=jnp.int32)
    allowed = (key_pos[None, :] >= query_start[:, None]) & (key_pos[None, :] <= query_pos[:, None])
    allowed = allowed[:, None, None, :]
    scores = jnp.where(allowed, scores, masked_score)
    new_max = jnp.maximum(run_max, jnp.max(scores, axis=-1))
    weights = jnp.where(allowed, jnp.exp(scores - new_max[..., None]), 0.0)
    factor = jnp.exp(run_max - new_max)
    run_sum = run_sum * factor + jnp.sum(weights, axis=-1)
    accumulated = accumulated * factor[..., None] + jnp.einsum(
        "tkgs,skd->tkgd",
        weights.astype(jnp.bfloat16),
        local_values,
        preferred_element_type=jnp.float32,
    )
    return (new_max, run_sum, accumulated)


def visit_block(state_now, block_slice, key_start, grouped_heads, query_pos, query_start):
    return fold_block(state_now, block_slice, key_start, grouped_heads, query_pos, query_start)


def per_device(rotated_queries, key_rows, value_matrix, doc_lengths):
    count_of_rows = rotated_queries.shape[0]
    span_count = lax.axis_size("ctx") // 2
    device_index = lax.axis_index("ctx")
    query_pos = device_index * count_of_rows + jnp.arange(count_of_rows, dtype=jnp.int32)
    query_start = doc_start_of(query_pos, doc_lengths)
    grouped_heads = rotated_queries.reshape(
        count_of_rows, KEY_VALUE_HEADS, QUERY_HEADS // KEY_VALUE_HEADS, HEAD_WIDTH
    )
    statistic_shape = (count_of_rows, KEY_VALUE_HEADS, QUERY_HEADS // KEY_VALUE_HEADS)
    state_now = (
        jnp.full(statistic_shape, masked_score, jnp.float32),
        jnp.zeros(statistic_shape, jnp.float32),
        jnp.zeros(statistic_shape + (HEAD_WIDTH,), jnp.float32),
    )
    own_block = jnp.stack([key_rows, value_matrix])
    state_now = visit_block(
        state_now, own_block, device_index * count_of_rows, grouped_heads, query_pos, query_start
    )
    stored = own_block[None]
    for level_number in range(16):
        held_count = stored.shape[0]
        send_count = min(held_count, span_count + 1 - held_count)
        if send_count > 0:
            arrived = from_behind(stored[:send_count], "ctx", held_count)

            def arrived_step(offset_number, inner_state, arrived=arrived, held_count=held_count):
                block_slice = lax.dynamic_index_in_dim(arrived, offset_number, 0, keepdims=False)
                key_start = (device_index - held_count - offset_number) * count_of_rows
                return visit_block(
                    inner_state, block_slice, key_start, grouped_heads, query_pos, query_start
                )

            state_now = lax.fori_loop(0, send_count, arrived_step, state_now)
            stored = jnp.concatenate([stored, arrived], axis=0)
    run_max, run_sum, accumulated = state_now
    result = accumulated / run_sum[..., None]
    return result.reshape(count_of_rows, QUERY_HEADS * HEAD_WIDTH).astype(jnp.bfloat16)


MESH = pl.DeviceIdType.MESH
GROUP_HEADS = QUERY_HEADS // KEY_VALUE_HEADS
EXP2_SCALE = math.log2(math.e) / math.sqrt(HEAD_WIDTH)

(Z1, Z2, C0, C1, C2, YA, YB, CYA, CYB) = range(9)
HOPS = 9
HEADS_AT_ONCE = 2


def relay_kernel(
    lengths_hbm, q_hbm, k_hbm, v_hbm, o_hbm,
    lengths, held, q_rows, v_rows, q_cols, row_max, row_sum, total, o_rows,
    lengths_sem, k_sem, v_sem, q_sem, o_sem, send_sem, recv_sem,
):
    tokens = q_hbm.shape[0]
    lanes = GROUP_HEADS * tokens
    group = lax.axis_index("groups")
    me = lax.axis_index("ctx")
    z, y, c = me // 4, (me // 2) % 2, me % 2
    up, down = me + 4, me - 4
    across = me + 2 - 4 * y
    twin = me + 1 - 2 * c

    def place(device):
        return (group, device)

    def slot(behind, head, from_y, from_c, which):
        return held.at[behind, head, from_y, which, from_c]

    def k_copy(head):
        columns = pl.ds(head * HEAD_WIDTH, HEAD_WIDTH)
        return pltpu.make_async_copy(k_hbm.at[:, columns], held.at[0, head, y, 0, c], k_sem.at[head])

    def v_copy(head):
        columns = pl.ds(head * HEAD_WIDTH, HEAD_WIDTH)
        return pltpu.make_async_copy(v_hbm.at[:, columns], v_rows.at[head], v_sem.at[head])

    def hop(kind, head, which, source, target, device):
        return pltpu.make_async_remote_copy(
            src_ref=source, dst_ref=target, send_sem=send_sem.at[kind, head, which],
            recv_sem=recv_sem.at[kind, head, which], device_id=place(device), device_id_type=MESH,
        )

    def send(kind, head, which, behind, from_y, from_c, device, landing=None):
        landing = behind if landing is None else landing
        source = slot(behind, head, from_y, from_c, which)
        hop(kind, head, which, source, slot(landing, head, from_y, from_c, which), device).start()

    def arrived_one(kind, head, which, behind, from_y, from_c):
        here = slot(behind, head, from_y, from_c, which)
        hop(kind, head, which, here, here, twin).wait_recv()

    def arrived(kind, head, behind, from_y, from_c):
        for which in range(2):
            arrived_one(kind, head, which, behind, from_y, from_c)

    q_copy = pltpu.make_async_copy(q_hbm, q_rows, q_sem)
    lengths_copy = pltpu.make_async_copy(lengths_hbm, lengths, lengths_sem)
    for head in range(KEY_VALUE_HEADS):
        v_copy(head).start()
        k_copy(head).start()
    q_copy.start()
    lengths_copy.start()

    barrier = pltpu.get_barrier_semaphore()

    def greet(device):
        pl.semaphore_signal(barrier, inc=1, device_id=place(device), device_id_type=MESH)

    greet(twin)
    greet(across)

    @pl.when(z < 3)
    def _():
        greet(up)

    @pl.when(z > 0)
    def _():
        greet(down)

    for head in range(KEY_VALUE_HEADS):
        v_copy(head).wait()
        held[0, head, y, 1, c] = v_rows[head].astype(jnp.float32).T.astype(jnp.bfloat16)

    inner = (z > 0) & (z < 3)

    @pl.when(inner)
    def _():
        pl.semaphore_wait(barrier, 4)

    @pl.when(jnp.logical_not(inner))
    def _():
        pl.semaphore_wait(barrier, 3)

    for head in range(KEY_VALUE_HEADS):
        k_copy(head).wait()

        for which in range(2):
            @pl.when(z < 3)
            def _():
                send(Z1, head, which, 0, y, c, up, landing=1)

            @pl.when(y == 0)
            def _():
                send(YA, head, which, 0, y, c, across)

            @pl.when(c == 0)
            def _():
                send(C0, head, which, 0, y, c, twin)

    lengths_copy.wait()
    q_copy.wait()
    for head in range(QUERY_HEADS):
        rows = q_rows[:, head * HEAD_WIDTH:(head + 1) * HEAD_WIDTH].astype(jnp.float32)
        at = head % GROUP_HEADS
        q_cols[head // GROUP_HEADS, :, at * tokens:(at + 1) * tokens] = rows.T.astype(jnp.bfloat16)

    query_pos = me * tokens + lax.broadcasted_iota(jnp.int32, (1, lanes), 1) % tokens
    doc_end = jnp.int32(0)
    query_start = jnp.zeros((1, lanes), jnp.int32)
    for doc in range(lengths.shape[0]):
        doc_end = doc_end + lengths[doc]
        query_start = query_start + jnp.where(doc_end <= query_pos, lengths[doc], 0)

    half = lanes // 2
    chains = [(at, part) for at in range(HEADS_AT_ONCE) for part in range(2)]

    def attend(heads, behind, from_y, from_c, first=False):
        count = tokens if from_c is not None else 2 * tokens
        key_start = ((z - behind) * 4 + from_y * 2 + (0 if from_c is None else from_c)) * tokens
        key_pos = lax.broadcasted_iota(jnp.int32, (count, half), 0)

        def cols_of(part):
            return slice(part * half, (part + 1) * half)

        def scores_of(chain):
            at, part = chain
            if from_c is None:
                keys = held[behind, heads + at, from_y, 0].reshape(count, HEAD_WIDTH)
            else:
                keys = held[behind, heads + at, from_y, 0, from_c]
            return jnp.dot(keys, q_cols[heads + at, :, cols_of(part)], preferred_element_type=jnp.float32)

        def top_of(chain, scores):
            at, part = chain
            cols = cols_of(part)
            allowed = key_pos >= query_start[:, cols] - key_start
            if first:
                allowed = allowed & (key_pos <= query_pos[:, cols] - key_start)
            scores = jnp.where(allowed, scores, masked_score)
            best, rows = scores, count
            while rows > 8:
                rows //= 2
                best = jnp.maximum(best[:rows], best[rows:])
            return scores, jnp.max(best, axis=0, keepdims=True)

        def values_of(chain):
            head = heads + chain[0]
            if from_c is None:
                values = jnp.concatenate(
                    [held[behind, head, from_y, 1, 0], held[behind, head, from_y, 1, 1]], axis=1
                )
            else:
                values = held[behind, head, from_y, 1, from_c]
            return jnp.concatenate([values, jnp.ones((16, count), jnp.bfloat16)], axis=0)

        masked = [top_of(chain, scores_of(chain)) for chain in chains]
        highest, olds = [], []
        for (at, part), (scores, top) in zip(chains, masked):
            old_max = None if first else row_max[heads + at, :, cols_of(part)]
            olds.append(old_max)
            highest.append(top if first else jnp.maximum(old_max, top))
        weights = [
            jnp.exp2((scores - new_max) * EXP2_SCALE).astype(jnp.bfloat16)
            for (scores, _), new_max in zip(masked, highest)
        ]
        mixed = [
            jnp.dot(values_of(chain), weight, preferred_element_type=jnp.float32)
            for chain, weight in zip(chains, weights)
        ]
        for (at, part), old_max, new_max, mix in zip(chains, olds, highest, mixed):
            head, cols = heads + at, cols_of(part)
            if first:
                row_sum[head, :, cols] = mix[HEAD_WIDTH:HEAD_WIDTH + 1]
                total[head, :, cols] = mix[:HEAD_WIDTH]
            else:
                factor = jnp.exp2((old_max - new_max) * EXP2_SCALE)
                row_sum[head, :, cols] = row_sum[head, :, cols] * factor + mix[HEAD_WIDTH:HEAD_WIDTH + 1]
                total[head, :, cols] = total[head, :, cols] * factor + mix[:HEAD_WIDTH]
            row_max[head, :, cols] = new_max

    def each(heads, wait):
        for at in range(HEADS_AT_ONCE):
            wait(heads + at)

    def z_first(head):
        @pl.when(z >= 1)
        def _():
            for which in range(2):
                arrived_one(Z1, head, which, 1, y, c)

                @pl.when(z < 3)
                def _():
                    send(Z2, head, which, 1, y, c, up, landing=2)

                send(YB - y, head, which, 1, y, c, across)
                send(C1, head, which, 1, y, c, twin)

    def z_second(head):
        @pl.when(z >= 2)
        def _():
            for which in range(2):
                arrived_one(Z2, head, which, 2, y, c)

                @pl.when(y == 1)
                def _():
                    send(YB, head, which, 2, y, c, across)

                @pl.when(c == 1)
                def _():
                    send(C2, head, which, 2, y, c, twin)

    crosses_first, crosses_second = z + y >= 1, z + y >= 2

    def y_first(head):
        @pl.when(crosses_first)
        def _():
            for which in range(2):
                arrived_one(YA, head, which, 1 - y, 1 - y, c)
                send(CYA, head, which, 1 - y, 1 - y, c, twin)

    def y_second(head):
        @pl.when(crosses_second)
        def _():
            for which in range(2):
                arrived_one(YB, head, which, 2 - y, 1 - y, c)
                send(CYB, head, which, 2 - y, 1 - y, c, twin)

    def o_copy(head):
        columns = pl.ds(pl.multiple_of(head * lanes, lanes), lanes)
        return pltpu.make_async_copy(o_rows.at[head], o_hbm.at[:, columns], o_sem.at[head])

    @pl.loop(0, 2)
    def _(step):
        heads = step * HEADS_AT_ONCE

        @pl.when(c == 0)
        def _():
            attend(heads, 0, y, 0, first=True)

        @pl.when(c == 1)
        def _():
            each(heads, lambda head: arrived(C0, head, 0, y, 0))
            attend(heads, 0, y, None, first=True)

        z_first(step)

    y_first(0)

    @pl.loop(0, 2)
    def _(step):
        heads = step * HEADS_AT_ONCE

        @pl.when(step == 0)
        def _():
            z_first(2)
            y_first(1)

        @pl.when(step == 1)
        def _():
            y_first(3)

        @pl.when(z >= 1)
        def _():
            each(heads, lambda head: arrived(C1, head, 1, y, 1 - c))
            attend(heads, 1, y, None)

        @pl.when(step == 0)
        def _():
            z_first(3)
            y_first(2)

        @pl.when(step == 1)
        def _():
            z_second(0)

        @pl.when(crosses_first)
        def _():
            each(heads, lambda head: arrived(CYA, head, 1 - y, 1 - y, 1 - c))
            attend(heads, 1 - y, 1 - y, None)

    z_second(1)
    y_second(0)
    z_second(2)
    y_second(1)

    @pl.loop(0, 2)
    def _(step):
        heads = step * HEADS_AT_ONCE

        @pl.when((z >= 2) & (c == 0))
        def _():
            each(heads, lambda head: arrived(C2, head, 2, y, 1))
            attend(heads, 2, y, None)

        @pl.when((z >= 2) & (c == 1))
        def _():
            attend(heads, 2, y, 1)

        @pl.when(step == 0)
        def _():
            z_second(3)
            y_second(2)

        @pl.when(step == 1)
        def _():
            y_second(3)

        @pl.when(crosses_second)
        def _():
            each(heads, lambda head: arrived(CYB, head, 2 - y, 1 - y, 1 - c))
            attend(heads, 2 - y, 1 - y, None)

        for at in range(HEADS_AT_ONCE):
            head = heads + at
            result = total[head] * (1.0 / row_sum[head])
            for own in range(GROUP_HEADS):
                own_cols = slice(own * tokens, (own + 1) * tokens)
                columns = slice(own * HEAD_WIDTH, (own + 1) * HEAD_WIDTH)
                o_rows[head, :, columns] = result[:, own_cols].astype(jnp.bfloat16).T
            o_copy(head).start()

    @pl.loop(0, KEY_VALUE_HEADS)
    def _(head):
        o_copy(head).wait()

        def sent(kind, behind, from_y, from_c):
            for which in range(2):
                here = slot(behind, head, from_y, from_c, which)
                hop(kind, head, which, here, here, twin).wait_send()

        @pl.when(z < 3)
        def _():
            sent(Z1, 0, y, c)

        @pl.when(c == 0)
        def _():
            sent(C0, 0, y, c)

        @pl.when(z - y >= 0)
        def _():
            sent(YA, y, y, c)

        @pl.when(z - y >= 1)
        def _():
            sent(YB, 1 + y, y, c)

        @pl.when(crosses_first)
        def _():
            sent(CYA, 1 - y, 1 - y, c)

        @pl.when(crosses_second)
        def _():
            sent(CYB, 2 - y, 1 - y, c)

        @pl.when(z >= 1)
        def _():
            sent(C1, 1, y, c)

            @pl.when(z < 3)
            def _():
                sent(Z2, 1, y, c)

        @pl.when((z >= 2) & (c == 1))
        def _():
            sent(C2, 2, y, c)


def relay_attention(rotated_queries, key_rows, value_matrix, doc_lengths):
    tokens = rotated_queries.shape[0]
    lanes = GROUP_HEADS * tokens
    in_hbm = pl.BlockSpec(memory_space=pl.ANY)
    pairs = 9 * tokens * tokens * QUERY_HEADS
    return pl.pallas_call(
        relay_kernel,
        out_shape=pltpu.VMEM(rotated_queries.shape, jnp.bfloat16),
        in_specs=[in_hbm] * 4,
        out_specs=pl.BlockSpec(memory_space=pl.ANY),
        scratch_shapes=[
            pltpu.SMEM(doc_lengths.shape, jnp.int32),
            pltpu.VMEM((3, KEY_VALUE_HEADS, 2, 2, 2, tokens, HEAD_WIDTH), jnp.bfloat16),
            pltpu.VMEM(rotated_queries.shape, jnp.bfloat16),
            pltpu.VMEM((KEY_VALUE_HEADS, tokens, HEAD_WIDTH), jnp.bfloat16),
            pltpu.VMEM((KEY_VALUE_HEADS, HEAD_WIDTH, lanes), jnp.bfloat16),
            pltpu.VMEM((KEY_VALUE_HEADS, 1, lanes), jnp.float32),
            pltpu.VMEM((KEY_VALUE_HEADS, 1, lanes), jnp.float32),
            pltpu.VMEM((KEY_VALUE_HEADS, HEAD_WIDTH, lanes), jnp.float32),
            pltpu.VMEM((KEY_VALUE_HEADS, tokens, GROUP_HEADS * HEAD_WIDTH), jnp.bfloat16),
            pltpu.SemaphoreType.DMA,
            pltpu.SemaphoreType.DMA((KEY_VALUE_HEADS,)),
            pltpu.SemaphoreType.DMA((KEY_VALUE_HEADS,)),
            pltpu.SemaphoreType.DMA,
            pltpu.SemaphoreType.DMA((KEY_VALUE_HEADS,)),
            pltpu.SemaphoreType.DMA((HOPS, KEY_VALUE_HEADS, 2)),
            pltpu.SemaphoreType.DMA((HOPS, KEY_VALUE_HEADS, 2)),
        ],
        compiler_params=pltpu.CompilerParams(
            collective_id=0, has_side_effects=True, vmem_limit_bytes=60 * 1024 * 1024
        ),
        cost_estimate=pl.CostEstimate(
            flops=4 * pairs * HEAD_WIDTH, bytes_accessed=4 * 1024 * 1024, transcendentals=pairs
        ),
        name="relay_attention",
    )(doc_lengths, rotated_queries, key_rows, value_matrix)


def solution(mesh):
    in_specs = (
        P(("groups", "ctx"), None),
        P(("groups", "ctx"), None),
        P(("groups", "ctx"), None),
        P("groups"),
    )
    out_specs = P(("groups", "ctx"), None)
    body = relay_attention if mesh.shape["ctx"] == 16 else per_device
    return jax.shard_map(
        body, mesh=mesh, in_specs=in_specs, out_specs=out_specs, check_vma=False
    )
```

```python
import math

import jax
import jax.numpy as jnp
from jax import lax
from jax.experimental import pallas as pl
from jax.experimental.pallas import tpu as pltpu
from jax.sharding import PartitionSpec as P

QUERY_HEADS = 16
KEY_VALUE_HEADS = 4
HEAD_WIDTH = 128


masked_score = -1e30


def from_behind(shard, axis, by):
    peers = lax.axis_size(axis)
    pairs = [(i, i + by) for i in range(peers) if 0 <= i + by < peers]
    return lax.ppermute(shard, axis, pairs)


def doc_start_of(query_pos, doc_lengths):
    doc_ends = jnp.cumsum(doc_lengths)
    taken_lengths = jnp.where(doc_ends[None, :] <= query_pos[:, None], doc_lengths[None, :], 0)
    return jnp.sum(taken_lengths, axis=1)


def fold_block(state_now, block_slice, key_start, grouped_heads, query_pos, query_start):
    run_max, run_sum, accumulated = state_now
    token_count = block_slice.shape[1]
    local_keys = block_slice[0].reshape(token_count, KEY_VALUE_HEADS, HEAD_WIDTH)
    local_values = block_slice[1].reshape(token_count, KEY_VALUE_HEADS, HEAD_WIDTH)
    scores = jnp.einsum(
        "tkgd,skd->tkgs", grouped_heads, local_keys, preferred_element_type=jnp.float32
    ) * HEAD_WIDTH ** (-0.5)
    key_pos = key_start + jnp.arange(token_count, dtype=jnp.int32)
    allowed = (key_pos[None, :] >= query_start[:, None]) & (key_pos[None, :] <= query_pos[:, None])
    allowed = allowed[:, None, None, :]
    scores = jnp.where(allowed, scores, masked_score)
    new_max = jnp.maximum(run_max, jnp.max(scores, axis=-1))
    weights = jnp.where(allowed, jnp.exp(scores - new_max[..., None]), 0.0)
    factor = jnp.exp(run_max - new_max)
    run_sum = run_sum * factor + jnp.sum(weights, axis=-1)
    accumulated = accumulated * factor[..., None] + jnp.einsum(
        "tkgs,skd->tkgd",
        weights.astype(jnp.bfloat16),
        local_values,
        preferred_element_type=jnp.float32,
    )
    return (new_max, run_sum, accumulated)


def visit_block(state_now, block_slice, key_start, grouped_heads, query_pos, query_start):
    return fold_block(state_now, block_slice, key_start, grouped_heads, query_pos, query_start)


def per_device(rotated_queries, key_rows, value_matrix, doc_lengths):
    count_of_rows = rotated_queries.shape[0]
    span_count = lax.axis_size("ctx") // 2
    device_index = lax.axis_index("ctx")
    query_pos = device_index * count_of_rows + jnp.arange(count_of_rows, dtype=jnp.int32)
    query_start = doc_start_of(query_pos, doc_lengths)
    grouped_heads = rotated_queries.reshape(
        count_of_rows, KEY_VALUE_HEADS, QUERY_HEADS // KEY_VALUE_HEADS, HEAD_WIDTH
    )
    statistic_shape = (count_of_rows, KEY_VALUE_HEADS, QUERY_HEADS // KEY_VALUE_HEADS)
    state_now = (
        jnp.full(statistic_shape, masked_score, jnp.float32),
        jnp.zeros(statistic_shape, jnp.float32),
        jnp.zeros(statistic_shape + (HEAD_WIDTH,), jnp.float32),
    )
    own_block = jnp.stack([key_rows, value_matrix])
    state_now = visit_block(
        state_now, own_block, device_index * count_of_rows, grouped_heads, query_pos, query_start
    )
    stored = own_block[None]
    for level_number in range(16):
        held_count = stored.shape[0]
        send_count = min(held_count, span_count + 1 - held_count)
        if send_count > 0:
            arrived = from_behind(stored[:send_count], "ctx", held_count)

            def arrived_step(offset_number, inner_state, arrived=arrived, held_count=held_count):
                block_slice = lax.dynamic_index_in_dim(arrived, offset_number, 0, keepdims=False)
                key_start = (device_index - held_count - offset_number) * count_of_rows
                return visit_block(
                    inner_state, block_slice, key_start, grouped_heads, query_pos, query_start
                )

            state_now = lax.fori_loop(0, send_count, arrived_step, state_now)
            stored = jnp.concatenate([stored, arrived], axis=0)
    run_max, run_sum, accumulated = state_now
    result = accumulated / run_sum[..., None]
    return result.reshape(count_of_rows, QUERY_HEADS * HEAD_WIDTH).astype(jnp.bfloat16)


MESH = pl.DeviceIdType.MESH
GROUP_HEADS = QUERY_HEADS // KEY_VALUE_HEADS
EXP2_SCALE = math.log2(math.e) / math.sqrt(HEAD_WIDTH)

(Z1, Z2, C0, C1, C2, YA, YB, CYA, CYB) = range(9)
HOPS = 9
HEADS_AT_ONCE = 2


def relay_kernel(
    lengths_hbm, q_hbm, k_hbm, v_hbm, o_ref,
    lengths, held, q_rows, v_rows, q_cols, row_max, row_sum, total,
    lengths_sem, k_sem, v_sem, q_sem, send_sem, recv_sem,
):
    tokens = q_hbm.shape[0]
    lanes = GROUP_HEADS * tokens
    group = lax.axis_index("groups")
    me = lax.axis_index("ctx")
    z, y, c = me // 4, (me // 2) % 2, me % 2
    up, down = me + 4, me - 4
    across = me + 2 - 4 * y
    twin = me + 1 - 2 * c

    def place(device):
        return (group, device)

    def slot(behind, head, from_y, from_c):
        return held.at[behind, head, from_y, :, from_c]

    def k_copy(head):
        columns = pl.ds(head * HEAD_WIDTH, HEAD_WIDTH)
        return pltpu.make_async_copy(k_hbm.at[:, columns], held.at[0, head, y, 0, c], k_sem.at[head])

    def v_copy(head):
        columns = pl.ds(head * HEAD_WIDTH, HEAD_WIDTH)
        return pltpu.make_async_copy(v_hbm.at[:, columns], v_rows.at[head], v_sem.at[head])

    def hop(kind, head, source, target, device):
        return pltpu.make_async_remote_copy(
            src_ref=source, dst_ref=target, send_sem=send_sem.at[kind, head],
            recv_sem=recv_sem.at[kind, head], device_id=place(device), device_id_type=MESH,
        )

    def send(kind, head, behind, from_y, from_c, device, landing=None):
        landing = behind if landing is None else landing
        hop(kind, head, slot(behind, head, from_y, from_c), slot(landing, head, from_y, from_c), device).start()

    def arrived(kind, head, behind, from_y, from_c):
        here = slot(behind, head, from_y, from_c)
        hop(kind, head, here, here, twin).wait_recv()

    q_copy = pltpu.make_async_copy(q_hbm, q_rows, q_sem)
    lengths_copy = pltpu.make_async_copy(lengths_hbm, lengths, lengths_sem)
    for head in range(KEY_VALUE_HEADS):
        v_copy(head).start()
        k_copy(head).start()
    q_copy.start()
    lengths_copy.start()

    barrier = pltpu.get_barrier_semaphore()

    def greet(device):
        pl.semaphore_signal(barrier, inc=1, device_id=place(device), device_id_type=MESH)

    greet(twin)
    greet(across)

    @pl.when(z < 3)
    def _():
        greet(up)

    @pl.when(z > 0)
    def _():
        greet(down)

    for head in range(KEY_VALUE_HEADS):
        v_copy(head).wait()
        held[0, head, y, 1, c] = v_rows[head].astype(jnp.float32).T.astype(jnp.bfloat16)

    inner = (z > 0) & (z < 3)

    @pl.when(inner)
    def _():
        pl.semaphore_wait(barrier, 4)

    @pl.when(jnp.logical_not(inner))
    def _():
        pl.semaphore_wait(barrier, 3)

    for head in range(KEY_VALUE_HEADS):
        k_copy(head).wait()

        @pl.when(z < 3)
        def _():
            send(Z1, head, 0, y, c, up, landing=1)

        @pl.when(y == 0)
        def _():
            send(YA, head, 0, y, c, across)

        @pl.when(c == 0)
        def _():
            send(C0, head, 0, y, c, twin)

    lengths_copy.wait()
    q_copy.wait()
    for head in range(QUERY_HEADS):
        rows = q_rows[:, head * HEAD_WIDTH:(head + 1) * HEAD_WIDTH].astype(jnp.float32)
        at = head % GROUP_HEADS
        q_cols[head // GROUP_HEADS, :, at * tokens:(at + 1) * tokens] = rows.T.astype(jnp.bfloat16)

    query_pos = me * tokens + lax.broadcasted_iota(jnp.int32, (1, lanes), 1) % tokens
    doc_end = jnp.int32(0)
    query_start = jnp.zeros((1, lanes), jnp.int32)
    for doc in range(lengths.shape[0]):
        doc_end = doc_end + lengths[doc]
        query_start = query_start + jnp.where(doc_end <= query_pos, lengths[doc], 0)

    half = lanes // 2
    chains = [(at, part) for at in range(HEADS_AT_ONCE) for part in range(2)]

    def attend(heads, behind, from_y, from_c, first=False):
        count = tokens if from_c is not None else 2 * tokens
        key_start = ((z - behind) * 4 + from_y * 2 + (0 if from_c is None else from_c)) * tokens
        key_pos = lax.broadcasted_iota(jnp.int32, (count, half), 0)

        def cols_of(part):
            return slice(part * half, (part + 1) * half)

        def scores_of(chain):
            at, part = chain
            if from_c is None:
                keys = held[behind, heads + at, from_y, 0].reshape(count, HEAD_WIDTH)
            else:
                keys = held[behind, heads + at, from_y, 0, from_c]
            return jnp.dot(keys, q_cols[heads + at, :, cols_of(part)], preferred_element_type=jnp.float32)

        def top_of(chain, scores):
            at, part = chain
            cols = cols_of(part)
            allowed = key_pos >= query_start[:, cols] - key_start
            if first:
                allowed = allowed & (key_pos <= query_pos[:, cols] - key_start)
            scores = jnp.where(allowed, scores, masked_score)
            best, rows = scores, count
            while rows > 8:
                rows //= 2
                best = jnp.maximum(best[:rows], best[rows:])
            return scores, jnp.max(best, axis=0, keepdims=True)

        def values_of(chain):
            head = heads + chain[0]
            if from_c is None:
                values = jnp.concatenate(
                    [held[behind, head, from_y, 1, 0], held[behind, head, from_y, 1, 1]], axis=1
                )
            else:
                values = held[behind, head, from_y, 1, from_c]
            return jnp.concatenate([values, jnp.ones((16, count), jnp.bfloat16)], axis=0)

        masked = [top_of(chain, scores_of(chain)) for chain in chains]
        highest, olds = [], []
        for (at, part), (scores, top) in zip(chains, masked):
            old_max = None if first else row_max[heads + at, :, cols_of(part)]
            olds.append(old_max)
            highest.append(top if first else jnp.maximum(old_max, top))
        weights = [
            jnp.exp2((scores - new_max) * EXP2_SCALE).astype(jnp.bfloat16)
            for (scores, _), new_max in zip(masked, highest)
        ]
        mixed = [
            jnp.dot(values_of(chain), weight, preferred_element_type=jnp.float32)
            for chain, weight in zip(chains, weights)
        ]
        for (at, part), old_max, new_max, mix in zip(chains, olds, highest, mixed):
            head, cols = heads + at, cols_of(part)
            if first:
                row_sum[head, :, cols] = mix[HEAD_WIDTH:HEAD_WIDTH + 1]
                total[head, :, cols] = mix[:HEAD_WIDTH]
            else:
                factor = jnp.exp2((old_max - new_max) * EXP2_SCALE)
                row_sum[head, :, cols] = row_sum[head, :, cols] * factor + mix[HEAD_WIDTH:HEAD_WIDTH + 1]
                total[head, :, cols] = total[head, :, cols] * factor + mix[:HEAD_WIDTH]
            row_max[head, :, cols] = new_max

    def each(heads, wait):
        for at in range(HEADS_AT_ONCE):
            wait(heads + at)

    def z_first(head):
        @pl.when(z >= 1)
        def _():
            arrived(Z1, head, 1, y, c)

            @pl.when(z < 3)
            def _():
                send(Z2, head, 1, y, c, up, landing=2)

            send(YB - y, head, 1, y, c, across)
            send(C1, head, 1, y, c, twin)

    def z_second(head):
        @pl.when(z >= 2)
        def _():
            arrived(Z2, head, 2, y, c)

            @pl.when(y == 1)
            def _():
                send(YB, head, 2, y, c, across)

            @pl.when(c == 1)
            def _():
                send(C2, head, 2, y, c, twin)

    crosses_first, crosses_second = z + y >= 1, z + y >= 2

    def y_first(head):
        @pl.when(crosses_first)
        def _():
            arrived(YA, head, 1 - y, 1 - y, c)
            send(CYA, head, 1 - y, 1 - y, c, twin)

    def y_second(head):
        @pl.when(crosses_second)
        def _():
            arrived(YB, head, 2 - y, 1 - y, c)
            send(CYB, head, 2 - y, 1 - y, c, twin)

    @pl.loop(0, 2)
    def _(step):
        heads = step * HEADS_AT_ONCE

        @pl.when(c == 0)
        def _():
            attend(heads, 0, y, 0, first=True)

        @pl.when(c == 1)
        def _():
            each(heads, lambda head: arrived(C0, head, 0, y, 0))
            attend(heads, 0, y, None, first=True)

        z_first(step)

    y_first(0)

    @pl.loop(0, 2)
    def _(step):
        heads = step * HEADS_AT_ONCE

        @pl.when(step == 0)
        def _():
            z_first(2)
            y_first(1)

        @pl.when(step == 1)
        def _():
            y_first(3)

        @pl.when(z >= 1)
        def _():
            each(heads, lambda head: arrived(C1, head, 1, y, 1 - c))
            attend(heads, 1, y, None)

        @pl.when(step == 0)
        def _():
            z_first(3)
            y_first(2)

        @pl.when(step == 1)
        def _():
            z_second(0)

        @pl.when(crosses_first)
        def _():
            each(heads, lambda head: arrived(CYA, head, 1 - y, 1 - y, 1 - c))
            attend(heads, 1 - y, 1 - y, None)

    z_second(1)
    y_second(0)
    z_second(2)
    y_second(1)

    @pl.loop(0, 2)
    def _(step):
        heads = step * HEADS_AT_ONCE

        @pl.when((z >= 2) & (c == 0))
        def _():
            each(heads, lambda head: arrived(C2, head, 2, y, 1))
            attend(heads, 2, y, None)

        @pl.when((z >= 2) & (c == 1))
        def _():
            attend(heads, 2, y, 1)

        @pl.when(step == 0)
        def _():
            z_second(3)
            y_second(2)

        @pl.when(step == 1)
        def _():
            y_second(3)

        @pl.when(crosses_second)
        def _():
            each(heads, lambda head: arrived(CYB, head, 2 - y, 1 - y, 1 - c))
            attend(heads, 2 - y, 1 - y, None)

        for at in range(HEADS_AT_ONCE):
            head = heads + at
            result = total[head] * (1.0 / row_sum[head])
            for own in range(GROUP_HEADS):
                own_cols = slice(own * tokens, (own + 1) * tokens)
                first_column = pl.multiple_of((head * GROUP_HEADS + own) * HEAD_WIDTH, HEAD_WIDTH)
                o_ref[:, pl.ds(first_column, HEAD_WIDTH)] = result[:, own_cols].astype(jnp.bfloat16).T

    @pl.loop(0, KEY_VALUE_HEADS)
    def _(head):
        def sent(kind, behind, from_y, from_c):
            here = slot(behind, head, from_y, from_c)
            hop(kind, head, here, here, twin).wait_send()

        @pl.when(z < 3)
        def _():
            sent(Z1, 0, y, c)

        @pl.when(c == 0)
        def _():
            sent(C0, 0, y, c)

        @pl.when(z - y >= 0)
        def _():
            sent(YA, y, y, c)

        @pl.when(z - y >= 1)
        def _():
            sent(YB, 1 + y, y, c)

        @pl.when(crosses_first)
        def _():
            sent(CYA, 1 - y, 1 - y, c)

        @pl.when(crosses_second)
        def _():
            sent(CYB, 2 - y, 1 - y, c)

        @pl.when(z >= 1)
        def _():
            sent(C1, 1, y, c)

            @pl.when(z < 3)
            def _():
                sent(Z2, 1, y, c)

        @pl.when((z >= 2) & (c == 1))
        def _():
            sent(C2, 2, y, c)


def relay_attention(rotated_queries, key_rows, value_matrix, doc_lengths):
    tokens = rotated_queries.shape[0]
    lanes = GROUP_HEADS * tokens
    in_hbm = pl.BlockSpec(memory_space=pl.ANY)
    pairs = 9 * tokens * tokens * QUERY_HEADS
    return pl.pallas_call(
        relay_kernel,
        out_shape=pltpu.VMEM(rotated_queries.shape, jnp.bfloat16),
        in_specs=[in_hbm] * 4,
        out_specs=pl.BlockSpec(memory_space=pltpu.VMEM),
        scratch_shapes=[
            pltpu.SMEM(doc_lengths.shape, jnp.int32),
            pltpu.VMEM((3, KEY_VALUE_HEADS, 2, 2, 2, tokens, HEAD_WIDTH), jnp.bfloat16),
            pltpu.VMEM(rotated_queries.shape, jnp.bfloat16),
            pltpu.VMEM((KEY_VALUE_HEADS, tokens, HEAD_WIDTH), jnp.bfloat16),
            pltpu.VMEM((KEY_VALUE_HEADS, HEAD_WIDTH, lanes), jnp.bfloat16),
            pltpu.VMEM((KEY_VALUE_HEADS, 1, lanes), jnp.float32),
            pltpu.VMEM((KEY_VALUE_HEADS, 1, lanes), jnp.float32),
            pltpu.VMEM((KEY_VALUE_HEADS, HEAD_WIDTH, lanes), jnp.float32),
            pltpu.SemaphoreType.DMA,
            pltpu.SemaphoreType.DMA((KEY_VALUE_HEADS,)),
            pltpu.SemaphoreType.DMA((KEY_VALUE_HEADS,)),
            pltpu.SemaphoreType.DMA,
            pltpu.SemaphoreType.DMA((HOPS, KEY_VALUE_HEADS)),
            pltpu.SemaphoreType.DMA((HOPS, KEY_VALUE_HEADS)),
        ],
        compiler_params=pltpu.CompilerParams(
            collective_id=0, has_side_effects=True, vmem_limit_bytes=60 * 1024 * 1024
        ),
        cost_estimate=pl.CostEstimate(
            flops=4 * pairs * HEAD_WIDTH, bytes_accessed=4 * 1024 * 1024, transcendentals=pairs
        ),
        name="relay_attention",
    )(doc_lengths, rotated_queries, key_rows, value_matrix)


def solution(mesh):
    in_specs = (
        P(("groups", "ctx"), None),
        P(("groups", "ctx"), None),
        P(("groups", "ctx"), None),
        P("groups"),
    )
    out_specs = P(("groups", "ctx"), None)
    body = relay_attention if mesh.shape["ctx"] == 16 else per_device
    return jax.shard_map(
        body, mesh=mesh, in_specs=in_specs, out_specs=out_specs, check_vma=False
    )
```
